128 devices in a mesh: row: 16 (over y, z_lo, core), col: 8 (over x, z_hi).
Axes of the slice: x: 4, y: 4, z: 4 (z_hi: 2, z_lo: 2; z = z_hi * 2 + z_lo), core: 2. Of those that a mesh axis runs over, the one named last changes fastest.
Arguments:
- matrix: float32 [16384, 16384], P('row', 'col'), may hold values from -8 to 8, as said below
- vectors: float32 [16384, 8192], P('row', 'col'), may hold values from -6 to 6
Outputs:
- updated: float32 [16384, 16384], P('row', 'col')
- rotated: float32 [16384, 8192], P('row', 'col')
The draws below stay inside these ranges and needn't reach their ends.
Inputs may be any that keep to these rules, and one draw needn't show every extreme that they name: matrix is symmetric up to rounding.
All inputs are finite; a program needn't handle non-finite values.
Results may differ from the reference program's by a relative error of at most 0.00011.
Values sent between devices are 32-bit elements; how exact they have to be, the bound alone decides.
No kernel may reach another device: no remote copies, remote signals or barrier semaphores. Data moves between devices by JAX's collectives and lax.ppermute only.
A program may use at most 128 MiB of HBM per device.

```python
import jax
import jax.numpy as jnp
from jax import lax

M = 16384
B = 256
NE = 8192


def draw_matrix(key, part):
    first_key = jax.random.fold_in(key, 11)
    normal_draw = jax.random.normal(first_key, (M, M), jnp.float32)
    symmetric = (normal_draw + normal_draw.T) * 0.7071067811865476
    return jnp.clip(symmetric, -8.0, 8.0)


def level_of(own_key, dims, cuts, low, high):
    loudness, own = 1.0, jax.random.fold_in(own_key, 6)
    for dim, shards_of in cuts:
        heights = jnp.exp(jax.random.uniform(jax.random.fold_in(own, dim), (shards_of,), jnp.float32, low / len(cuts), high / len(cuts)))
        loudness = loudness * jnp.repeat(heights, dims[dim] // shards_of).reshape([-1 if axis == dim else 1 for axis in range(len(dims))])
    return loudness


def centred(own_key, shape, deviation, limit, shards=(), held_as=jnp.bfloat16):
    array = jax.random.normal(own_key, shape, jnp.float32) * deviation
    if len(shards) > 0:
        array = level_of(own_key, shape, shards, -0.22, 0.18) * array
    return jnp.clip(array, min=-limit, max=limit).astype(held_as)


def setup_inputs(seed: int = 0) -> dict:
    keys = jax.random.split(jax.random.key(seed), 3)
    return {
        "matrix": draw_matrix(jax.random.fold_in(keys[2], 71), 0),
        "vectors": centred(keys[1], (M, NE), 1.0, 6.0, ((0, 16), (1, 8)), jnp.float32),
    }


def matmul(left, right):
    return jnp.dot(left.astype(jnp.float32), right.astype(jnp.float32), preferred_element_type=jnp.float32, precision=lax.Precision.HIGHEST)

def reference(matrix, vectors):
    row_ids = jnp.arange(M, dtype=jnp.int32)
    panel = jnp.where(row_ids[:, None] >= B, matrix[:, :B], jnp.float32(0.0))
    gram = matmul(panel.T, panel)
    factor = jnp.linalg.cholesky(gram)
    basis = lax.linalg.triangular_solve(factor, panel, left_side=False, lower=True, transpose_a=True)
    product = matmul(matrix, basis)
    coupling = matmul(basis.T, product)
    wide = 2.0 * product - 2.0 * matmul(basis, coupling)
    updated = matrix - matmul(basis, wide.T) - matmul(wide, basis.T)
    mixing = matmul(basis.T, vectors)
    rotated = vectors - 2.0 * matmul(basis, mixing)
    return (updated, rotated)
```

```python
import jax
import jax.numpy as jnp
from jax import lax
from jax.experimental import pallas as pl
from jax.experimental.pallas import tpu as pltpu
from jax.sharding import Mesh
from jax.sharding import PartitionSpec as P

B = 256
ROW = ("y", "zl", "co")
CHIPS = ("y", "zl")
COL = ("x", "zh")
ALL = ("y", "zl", "co", "x", "zh")
HIGH = lax.Precision.HIGH
HIGHEST = lax.Precision.HIGHEST


def nn(left, right, precision=HIGH):
    return lax.dot_general(
        left, right, (((1,), (0,)), ((), ())), preferred_element_type=jnp.float32, precision=precision
    )


def tn(left, right, precision=HIGH):
    return lax.dot_general(
        left, right, (((0,), (0,)), ((), ())), preferred_element_type=jnp.float32, precision=precision
    )


def nt(left, right, precision=HIGH):
    return lax.dot_general(
        left, right, (((1,), (1,)), ((), ())), preferred_element_type=jnp.float32, precision=precision
    )


def sweep_all(block):
    n, group = 128, 16
    lane = lax.broadcasted_iota(jnp.int32, (1, n), 1)
    line = lax.broadcasted_iota(jnp.int32, (n, 1), 0)

    def step(_, s):
        for k in range(0, group, 2):
            r0, r1 = s[k : k + 1, :], s[k + 1 : k + 2, :]
            c0, c1 = s[:, k : k + 1], s[:, k + 1 : k + 2]
            a, b, d = r0[:, k : k + 1], r0[:, k + 1 : k + 2], r1[:, k + 1 : k + 2]
            scale = 1.0 / (a * d - b * b)
            ia, ib, id_ = d * scale, -b * scale, a * scale
            q0 = ia * r0 + ib * r1
            q1 = ib * r0 + id_ * r1
            q0 = jnp.where(lane == k, -ia, jnp.where(lane == k + 1, -ib, q0))
            q1 = jnp.where(lane == k, -ib, jnp.where(lane == k + 1, -id_, q1))
            c0 = jnp.where(line == k, -1.0, jnp.where(line == k + 1, 0.0, c0))
            c1 = jnp.where(line == k, 0.0, jnp.where(line == k + 1, -1.0, c1))
            keep = ((lane != k) & (lane != k + 1)) & ((line != k) & (line != k + 1))
            s = jnp.where(keep, s, 0.0) - c0 * q0 - c1 * q1
        s = jnp.concatenate([s[group:], s[:group]], axis=0)
        return pltpu.roll(s, n - group, 1)

    return lax.fori_loop(0, n // group, step, block)


def invert_kernel(gram_ref, out_ref):
    h = B // 2
    a, b, d = gram_ref[:h, :h], gram_ref[:h, h:], gram_ref[h:, h:]
    ai = -sweep_all(a)
    t = nn(ai, b, HIGHEST)
    si = -sweep_all(d - tn(b, t, HIGHEST))
    u = nn(t, si, HIGHEST)
    out_ref[:h, :h] = ai + nt(u, t, HIGHEST)
    out_ref[:h, h:] = -u
    out_ref[h:, :h] = -u.T
    out_ref[h:, h:] = si


def invert(gram):
    return pl.pallas_call(
        invert_kernel,
        out_shape=jax.ShapeDtypeStruct((B, B), jnp.float32),
        cost_estimate=pl.CostEstimate(flops=2 * B**3 * 20, bytes_accessed=8 * B * B, transcendentals=0),
    )(gram)


def repeat(block, n):
    return jnp.broadcast_to(block[None], (n,) + block.shape)


def exchange(blocks, axes):
    return lax.all_to_all(blocks, axes, 0, 0, tiled=True)


def swap_cores(array):
    return lax.ppermute(array, "co", [(0, 1), (1, 0)])


def flip_pairs():
    pairs = []
    for i in range(16):
        for k in range(8):
            pairs.append((i * 8 + k, (k * 2 + i % 2) * 8 + i // 2))
    return pairs


def body(matrix, vectors):
    rows_here = matrix.shape[0]
    row_index = lax.axis_index(ROW)
    col_index = lax.axis_index(COL)
    core = lax.axis_index("co")
    there = flip_pairs()
    back = [(b, a) for a, b in there]

    global_rows = row_index * rows_here + jnp.arange(rows_here, dtype=jnp.int32)
    panel = jnp.where(global_rows[:, None] >= B, matrix[:, :B], jnp.float32(0.0))
    mine = panel[:128]
    for k in range(1, 8):
        got = lax.ppermute(panel[k * 128 : (k + 1) * 128], COL, [(0, k)])
        mine = jnp.where(col_index == k, got, mine)
    mine_t = lax.ppermute(mine, ALL, there)

    panel_rows = exchange(repeat(mine, 8), COL).reshape(1024, B)
    half = exchange(repeat(mine_t, 8), CHIPS).reshape(1024, B)
    other = swap_cores(half)
    panel_cols = jnp.where(
        core == 0, jnp.concatenate([half, other]), jnp.concatenate([other, half])
    )

    product_t = tn(matrix, panel_rows)
    mixing_t = tn(vectors, panel_rows)
    gram = tn(panel_rows, panel_rows, HIGHEST)
    coupling = tn(panel_cols, product_t)
    parts = jnp.concatenate(
        [
            product_t.reshape(2, 8, 128, B),
            mixing_t.reshape(2, 8, 64, B),
            gram.reshape(2, 8, 16, B),
            coupling.reshape(2, 8, 16, B),
        ],
        axis=2,
    )
    keep = jnp.where(core == 0, parts[0], parts[1])
    give = jnp.where(core == 0, parts[1], parts[0])
    own = jnp.sum(exchange(keep + swap_cores(give), CHIPS), axis=0)

    coupling16 = jnp.sum(exchange(repeat(own[208:], 8), COL), axis=0)
    product_mine = lax.ppermute(own[:128], ALL, back)
    half = exchange(repeat(jnp.concatenate([own[:208], coupling16]), 8), CHIPS)
    product_rows = exchange(repeat(product_mine, 8), COL).reshape(1024, B)
    other = swap_cores(half)
    low = jnp.where(core == 0, half, other)
    high = jnp.where(core == 0, other, half)
    full = jnp.stack([low, high])
    product_cols = full[:, :, :128].reshape(2048, B)
    mixing_t = full[:, :, 128:192].reshape(1024, B)
    gram = full[:, :, 192:208].reshape(B, B)
    coupling = full[:, :, 208:].reshape(B, B)

    inverse = invert(gram)
    u1 = 2.0 * nn(panel_rows, inverse, HIGHEST)
    u2 = 2.0 * nn(product_rows, inverse, HIGHEST) - 2.0 * nn(u1, nn(coupling, inverse, HIGHEST), HIGHEST)
    rotated = vectors - nt(u1, mixing_t)
    updated = matrix - nt(jnp.concatenate([u1, u2], axis=1), jnp.concatenate([product_cols, panel_cols], axis=1))
    return (updated, rotated)


def solution(mesh):
    fine = Mesh(mesh.devices.reshape(4, 2, 2, 4, 2), ALL)
    placed = (P(ROW, COL), P(ROW, COL))
    return jax.shard_map(body, mesh=fine, in_specs=placed, out_specs=placed, check_vma=False)
```

```python
import jax
import jax.numpy as jnp
from jax import lax
from jax.experimental import pallas as pl
from jax.experimental.pallas import tpu as pltpu
from jax.sharding import Mesh
from jax.sharding import PartitionSpec as P

B = 256
ROW = ("y", "zl", "co")
CHIPS = ("y", "zl")
COL = ("x", "zh")
COUPLED = ("co", "x", "zh")
ALL = ("y", "zl", "co", "x", "zh")
HIGHEST = lax.Precision.HIGHEST
F32 = jnp.float32
BF16 = jnp.bfloat16
NN = (((1,), (0,)), ((), ()))
NT = (((1,), (1,)), ((), ()))
TN = (((0,), (0,)), ((), ()))


def dot(left, right, dims=NN):
    return lax.dot_general(left, right, dims, preferred_element_type=F32, precision=HIGHEST)


def split(x):
    hi = x.astype(BF16)
    return hi, (x - hi.astype(F32)).astype(BF16)


def dot3(left, right, dims=NN):
    (ah, al), (bh, bl) = left, right
    f = lambda a, b: lax.dot_general(a, b, dims, preferred_element_type=F32)
    return f(ah, bh) + (f(ah, bl) + f(al, bh))


def call(kernel, out_shape, us, mib=8, **kw):
    cost = pl.CostEstimate(flops=int(us * 1e9), bytes_accessed=1024, transcendentals=0)
    params = pltpu.CompilerParams(vmem_limit_bytes=mib * 1024 * 1024)
    return pl.pallas_call(kernel, out_shape=out_shape, cost_estimate=cost, compiler_params=params, **kw)


def f32(*shape):
    return jax.ShapeDtypeStruct(shape, F32)


def sweep_all(block):
    n, group = 128, 16
    lane = lax.broadcasted_iota(jnp.int32, (8, n), 1)
    line = lax.broadcasted_iota(jnp.int32, (8, n), 0)
    tiles = n // 8

    def step(_, s):
        s = list(s)
        for k in range(0, group, 2):
            t, sub = k // 8, k % 8
            r0 = jnp.broadcast_to(s[t][sub : sub + 1, :], (8, n))
            r1 = jnp.broadcast_to(s[t][sub + 1 : sub + 2, :], (8, n))
            a = jnp.broadcast_to(r0[:, k : k + 1], (8, n))
            b = jnp.broadcast_to(r1[:, k : k + 1], (8, n))
            d = jnp.broadcast_to(r1[:, k + 1 : k + 2], (8, n))
            scale = 1.0 / (a * d - b * b)
            ia, ib, ic = d * scale, -b * scale, a * scale
            q0 = jnp.where(lane == k, -ia, jnp.where(lane == k + 1, -ib, ia * r0 + ib * r1))
            q1 = jnp.where(lane == k, -ib, jnp.where(lane == k + 1, -ic, ib * r0 + ic * r1))
            pivots = (lane == k) | (lane == k + 1)
            for u in range(tiles):
                c0 = jnp.broadcast_to(s[u][:, k : k + 1], (8, n))
                c1 = jnp.broadcast_to(s[u][:, k + 1 : k + 2], (8, n))
                new = jnp.where(pivots, 0.0, s[u]) - c0 * q0 - c1 * q1
                if u == t:
                    new = jnp.where(line == sub, q0, jnp.where(line == sub + 1, q1, new))
                s[u] = new
        s = s[group // 8 :] + s[: group // 8]
        return tuple(pltpu.roll(v, n - group, 1) for v in s)

    out = lax.fori_loop(0, n // group, step, tuple(block[8 * u : 8 * u + 8, :] for u in range(tiles)))
    return jnp.concatenate(out, axis=0)


def invert_first(gram_ref, ai_ref, t_ref, schur_ref):
    def part(lo, lanes):
        return jnp.concatenate([gram_ref[m, 32 * lanes : 32 * lanes + 32, :] for m in range(lo, lo + 4)], axis=0)

    b = part(0, 1)
    ai = -sweep_all(part(0, 0))
    t = dot(ai, b)
    ai_ref[...] = ai
    t_ref[...] = t
    schur_ref[...] = part(4, 1) - dot(b, t, TN)


def invert_second(ai_ref, t_ref, schur_ref, out_ref):
    h = B // 2
    t = t_ref[...]
    si = -sweep_all(schur_ref[...])
    u = dot(t, si)
    out_ref[:h, :h] = ai_ref[...] + dot(u, t, NT)
    out_ref[:h, h:] = -u
    out_ref[h:, :h] = -u.T
    out_ref[h:, h:] = si


def choose_kernel(col_ref, *refs):
    parts, (out_ref, turned_ref) = refs[:8], refs[8:]
    mine = parts[0][...]
    for k in range(1, 8):
        mine = jnp.where(col_ref[0] == k, parts[k][...], mine)
    for k in range(8):
        out_ref[k] = mine
    turned_ref[...] = mine.T


def gram_kernel(panel_ref, out_ref):
    gram = dot(panel_ref[...].T, panel_ref[...]).reshape(8, 32, B)
    out_ref[:, :32, :] = gram[:, :, :128]
    out_ref[:, 32:, :] = gram[:, :, 128:]


def product_kernel(core_ref, panel_ref, matrix_ref, vectors_ref, keep_ref, give_ref, hi_ref, lo_ref):
    step = pl.program_id(0)
    core = core_ref[0]

    def put(own, both, place):
        @pl.when(own == core)
        def _():
            keep_ref[:, place, :] = both[0]
            give_ref[:, place, :] = both[1]

        @pl.when(own != core)
        def _():
            keep_ref[:, place, :] = both[1]
            give_ref[:, place, :] = both[0]

    @pl.when(step == 0)
    def _():
        hi_ref[...], lo_ref[...] = split(panel_ref[...].T)

    panel = hi_ref[...], lo_ref[...]
    product = dot3(panel, split(matrix_ref[...]))
    mixing = dot3(panel, split(vectors_ref[...])).reshape(2, 8, 16, 128)
    m = (2 * step) % 8
    put(0, mixing, pl.ds(pl.multiple_of(256 + 16 * step, 16), 16))

    @pl.when(step // 4 == core)
    def _():
        keep_ref[m, :256, :] = product[:, :128]
        keep_ref[m + 1, :256, :] = product[:, 128:]

    @pl.when(step // 4 != core)
    def _():
        give_ref[m, :256, :] = product[:, :128]
        give_ref[m + 1, :256, :] = product[:, 128:]


def join_kernel(keep_ref, got_ref, gram_ref, other_ref, out_ref):
    out_ref[:, :384, :] = keep_ref[...] + got_ref[...]
    gram = gram_ref[...] + other_ref[...]
    for m in range(8):
        out_ref[m, 384:, :] = gram


def reduce_kernel(in_ref, turned_ref, product_ref, gram_ref, out_ref):
    own = in_ref[0, :384, :]
    for m in range(1, 8):
        own = own + in_ref[m, :384, :]
    product_ref[...] = own[:256].T
    gram_ref[...] = in_ref[:, 384:, :]
    for m in range(8):
        out_ref[m, :384, :] = own
        out_ref[m, 384:, :] = turned_ref[...]


def coupling_kernel(panel_ref, product_ref, out_ref):
    total = jnp.zeros((B, B), F32)
    for m in range(0, 8, 2):
        left = jnp.concatenate([panel_ref[m], panel_ref[m + 1]], axis=1)
        right = jnp.concatenate([product_ref[m], product_ref[m + 1]], axis=1)
        total = total + dot3(split(left), split(right), NT)
    out_ref[...] = total.reshape(16, 16, B)


def sum_kernel(in_ref, out_ref):
    total = jnp.sum(in_ref[...], axis=0)
    for m in range(out_ref.shape[0]):
        out_ref[m] = total


def rotate_kernel(core_ref, panel_ref, inverse_ref, mine_ref, other_ref, vectors_ref, out_ref, u_ref, left_ref):
    @pl.when(pl.program_id(0) == 0)
    def _():
        u = 2.0 * dot(panel_ref[...], inverse_ref[...])
        u_ref[...] = u
        hi, lo = split(u)
        left_ref[:, :256], left_ref[:, 256:512], left_ref[:, 512:] = hi, hi, lo

    core = core_ref[0]
    mine, other = mine_ref[...], other_ref[...]
    both = jnp.where(core == 0, mine, other), jnp.where(core == 0, other, mine)
    lanes = [jnp.concatenate([h[:, k : k + 16, :].reshape(128, 128) for h in both], axis=0) for k in (0, 16)]
    hi, lo = split(jnp.concatenate(lanes, axis=1))
    right = jnp.concatenate([hi, lo, hi], axis=0)
    out_ref[...] = vectors_ref[...] - lax.dot_general(left_ref[...], right, NN, preferred_element_type=F32)


def update_kernel(
    where_ref, u_ref, near_ref, far_ref, inverse_ref, coupling_ref,
    mine_ref, other_ref, pmine_ref, pother_ref, matrix_ref, out_ref, left_ref, product_ref,
):
    step = pl.program_id(0)

    @pl.when(step == 0)
    def _():
        for k in range(4):
            for piece_ref, zh in ((near_ref, where_ref[2]), (far_ref, 1 - where_ref[2])):
                place = (lax.rem(where_ref[1] + k, 4) * 2 + zh) * 128
                product_ref[pl.ds(pl.multiple_of(place, 128), 128), :] = piece_ref[k]
        small = dot(coupling_ref[...].reshape(B, B), inverse_ref[...])
        u1 = u_ref[...]
        u2 = 2.0 * dot(product_ref[...], inverse_ref[...]) - 2.0 * dot(u1, small)
        for k, u in ((0, u1), (256, u2)):
            hi, lo = split(u)
            left_ref[:, k : k + 256], left_ref[:, k + 512 : k + 768], left_ref[:, k + 1024 : k + 1280] = hi, hi, lo

    mine = step // 4 == where_ref[0]
    product = jnp.where(mine, mine_ref[...], other_ref[...])
    panel = jnp.where(mine, pmine_ref[...], pother_ref[...])
    hi, lo = split(
        jnp.concatenate(
            [jnp.concatenate([product[0], product[1]], axis=1), jnp.concatenate([panel[0], panel[1]], axis=1)], axis=0
        )
    )
    right = jnp.concatenate([hi, lo, hi], axis=0)
    out_ref[...] = matrix_ref[...] - lax.dot_general(left_ref[...], right, NN, preferred_element_type=F32)


def repeat(block, n=8):
    return jnp.broadcast_to(block[None], (n,) + block.shape)


def exchange(blocks, axes):
    return lax.all_to_all(blocks, axes, 0, 0, tiled=True)


def swap_cores(array):
    return lax.ppermute(array, "co", [(0, 1), (1, 0)])


def gather_x(block):
    return jnp.stack([block] + [lax.ppermute(block, "x", [((x + k) % 4, x) for x in range(4)]) for k in (1, 2, 3)])


def flip_pairs():
    pairs = []
    for i in range(16):
        for k in range(8):
            pairs.append((i * 8 + k, (k * 2 + i % 2) * 8 + i // 2))
    return pairs


VMEM = pl.BlockSpec(memory_space=pltpu.VMEM)
SMEM = pl.BlockSpec(memory_space=pltpu.SMEM)


def whole(*shape):
    return pl.BlockSpec(shape, lambda t: (0,) * len(shape))


def body(matrix, vectors):
    rows_here = matrix.shape[0]
    row_index = lax.axis_index(ROW)
    col_index = lax.axis_index(COL)
    core = lax.axis_index("co").astype(jnp.int32).reshape(1)
    where = jnp.stack([core[0], lax.axis_index("x").astype(jnp.int32), lax.axis_index("zh").astype(jnp.int32)])
    there = flip_pairs()
    back = [(b, a) for a, b in there]

    global_rows = row_index * rows_here + jnp.arange(rows_here, dtype=jnp.int32)
    panel = jnp.where(global_rows[:, None] >= B, matrix[:, :B], F32(0.0))
    parts = [panel[:128]]
    for k in range(1, 8):
        parts.append(lax.ppermute(panel[k * 128 : (k + 1) * 128], COL, [(0, k)]))
    sent, turned = call(
        choose_kernel, (f32(8, 128, 256), f32(256, 128)), 1, in_specs=[SMEM] + [VMEM] * 8
    )(col_index.astype(jnp.int32).reshape(1), *parts)
    panel_rows, turned = lax.optimization_barrier((exchange(sent, COL).reshape(1024, B), turned))
    turned = lax.ppermute(turned, ALL, there)
    wide = whole(8, 384, 128)
    gram = exchange(call(gram_kernel, f32(8, 64, 128), 1)(panel_rows), CHIPS)
    keep, give = call(
        product_kernel,
        (f32(8, 384, 128), f32(8, 384, 128)),
        12,
        60,
        grid=(8,),
        in_specs=[
            SMEM,
            whole(1024, 256),
            pl.BlockSpec((1024, 256), lambda t: (0, t)),
            pl.BlockSpec((1024, 128), lambda t: (0, t)),
        ],
        out_specs=(wide, wide),
        scratch_shapes=[pltpu.VMEM((256, 1024), BF16), pltpu.VMEM((256, 1024), BF16)],
    )(core, panel_rows, matrix, vectors)
    keep, give, turned, gram = lax.optimization_barrier((keep, give, turned, gram))
    gram = jnp.sum(gram, axis=0)
    came = exchange(
        call(join_kernel, f32(8, 448, 128), 1, 12)(keep, swap_cores(give), gram, swap_cores(gram)), CHIPS
    )

    product, gram, sent = call(reduce_kernel, (f32(128, 256), f32(8, 64, 128), f32(8, 640, 128)), 2, 12)(came, turned)
    final = exchange(sent, CHIPS)
    near = gather_x(lax.ppermute(product, ALL, back))
    ai, t, schur = call(invert_first, (f32(128, 128),) * 3, 9)(gram)
    inverse = call(invert_second, f32(B, B), 9)(ai, t, schur)
    final, near, inverse = lax.optimization_barrier((final, near, inverse))
    other = swap_cores(final)
    far = lax.ppermute(near, "zh", [(0, 1), (1, 0)])
    coupling = call(
        coupling_kernel,
        f32(16, 16, 256),
        2,
        grid=(1,),
        in_specs=[
            pl.BlockSpec((pl.Element(8), pl.Element(256), pl.Element(128)), lambda t: (0, 384, 0)),
            pl.BlockSpec((8, 256, 128), lambda t: (0, 0, 0)),
        ],
        out_specs=whole(16, 16, 256),
    )(final, final)
    coupling = call(sum_kernel, f32(16, 16, 256), 1)(exchange(coupling, COUPLED))
    coupling = exchange(coupling, COUPLED)

    mixing = pl.BlockSpec((8, 32, 128), lambda t: (0, 8 + t, 0))
    rotated, u = call(
        rotate_kernel,
        (f32(1024, 1024), f32(1024, 256)),
        6,
        60,
        grid=(4,),
        in_specs=[
            SMEM, whole(1024, 256), whole(256, 256), mixing, mixing, pl.BlockSpec((1024, 256), lambda t: (0, t)),
        ],
        out_specs=(pl.BlockSpec((1024, 256), lambda t: (0, t)), whole(1024, 256)),
        scratch_shapes=[pltpu.VMEM((1024, 768), BF16)],
    )(core, panel_rows, inverse, final, other, vectors)

    coupling, rotated, u = lax.optimization_barrier((coupling, rotated, u))
    pair = pl.BlockSpec((2, 256, 128), lambda t: (t % 4, 0, 0))
    piece = whole(4, 128, 256)
    panel_pair = pl.BlockSpec((pl.Element(2), pl.Element(256), pl.Element(128)), lambda t: (2 * (t % 4), 384, 0))
    updated = call(
        update_kernel,
        f32(1024, 2048),
        12,
        60,
        grid=(8,),
        in_specs=[
            SMEM, whole(1024, 256), piece, piece, whole(256, 256), whole(16, 16, 256), pair, pair, panel_pair,
            panel_pair, pl.BlockSpec((1024, 256), lambda t: (0, t)),
        ],
        out_specs=pl.BlockSpec((1024, 256), lambda t: (0, t)),
        scratch_shapes=[pltpu.VMEM((1024, 1536), BF16), pltpu.VMEM((1024, 256), F32)],
    )(where, u, near, far, inverse, coupling, final, other, final, other, matrix)
    return (updated, rotated)


def solution(mesh):
    fine = Mesh(mesh.devices.reshape(4, 2, 2, 4, 2), ALL)
    placed = (P(ROW, COL), P(ROW, COL))
    return jax.shard_map(body, mesh=fine, in_specs=placed, out_specs=placed, check_vma=False)
```

```python
import jax
import jax.numpy as jnp
from jax import lax
from jax.experimental import pallas as pl
from jax.experimental.pallas import tpu as pltpu
from jax.sharding import Mesh
from jax.sharding import PartitionSpec as P

B = 256
ROW = ("y", "zl", "co")
CHIPS = ("y", "zl")
COL = ("x", "zh")
COUPLED = ("co", "x", "zh")
ALL = ("y", "zl", "co", "x", "zh")
HIGHEST = lax.Precision.HIGHEST
F32 = jnp.float32
BF16 = jnp.bfloat16
NN = (((1,), (0,)), ((), ()))
NT = (((1,), (1,)), ((), ()))
TN = (((0,), (0,)), ((), ()))


def dot(left, right, dims=NN):
    return lax.dot_general(left, right, dims, preferred_element_type=F32, precision=HIGHEST)


def split(x):
    hi = x.astype(BF16)
    return hi, (x - hi.astype(F32)).astype(BF16)


def dot3(left, right, dims=NN):
    (ah, al), (bh, bl) = left, right
    f = lambda a, b: lax.dot_general(a, b, dims, preferred_element_type=F32)
    return f(ah, bh) + (f(ah, bl) + f(al, bh))


def call(kernel, out_shape, us, mib=8, **kw):
    cost = pl.CostEstimate(flops=int(us * 1e9), bytes_accessed=1024, transcendentals=0)
    params = pltpu.CompilerParams(vmem_limit_bytes=mib * 1024 * 1024)
    return pl.pallas_call(kernel, out_shape=out_shape, cost_estimate=cost, compiler_params=params, **kw)


def f32(*shape):
    return jax.ShapeDtypeStruct(shape, F32)


def sweep_all(block):
    n, group = 128, 16
    lane = lax.broadcasted_iota(jnp.int32, (8, n), 1)
    line = lax.broadcasted_iota(jnp.int32, (8, n), 0)
    tiles = n // 8

    def step(_, s):
        s = list(s)
        for k in range(0, group, 2):
            t, sub = k // 8, k % 8
            r0 = jnp.broadcast_to(s[t][sub : sub + 1, :], (8, n))
            r1 = jnp.broadcast_to(s[t][sub + 1 : sub + 2, :], (8, n))
            a = jnp.broadcast_to(r0[:, k : k + 1], (8, n))
            b = jnp.broadcast_to(r1[:, k : k + 1], (8, n))
            d = jnp.broadcast_to(r1[:, k + 1 : k + 2], (8, n))
            scale = 1.0 / (a * d - b * b)
            ia, ib, ic = d * scale, -b * scale, a * scale
            q0 = jnp.where(lane == k, -ia, jnp.where(lane == k + 1, -ib, ia * r0 + ib * r1))
            q1 = jnp.where(lane == k, -ib, jnp.where(lane == k + 1, -ic, ib * r0 + ic * r1))
            pivots = (lane == k) | (lane == k + 1)
            for u in range(tiles):
                c0 = jnp.broadcast_to(s[u][:, k : k + 1], (8, n))
                c1 = jnp.broadcast_to(s[u][:, k + 1 : k + 2], (8, n))
                new = jnp.where(pivots, 0.0, s[u]) - c0 * q0 - c1 * q1
                if u == t:
                    new = jnp.where(line == sub, q0, jnp.where(line == sub + 1, q1, new))
                s[u] = new
        s = s[group // 8 :] + s[: group // 8]
        return tuple(pltpu.roll(v, n - group, 1) for v in s)

    out = lax.fori_loop(0, n // group, step, tuple(block[8 * u : 8 * u + 8, :] for u in range(tiles)))
    return jnp.concatenate(out, axis=0)


def invert_first(gram_ref, ai_ref, t_ref, schur_ref):
    def part(lo, lanes):
        return jnp.concatenate([gram_ref[m, 32 * lanes : 32 * lanes + 32, :] for m in range(lo, lo + 4)], axis=0)

    b = part(0, 1)
    ai = -sweep_all(part(0, 0))
    t = dot(ai, b)
    ai_ref[...] = ai
    t_ref[...] = t
    schur_ref[...] = part(4, 1) - dot(b, t, TN)


def invert_second(ai_ref, t_ref, schur_ref, out_ref):
    h = B // 2
    t = t_ref[...]
    si = -sweep_all(schur_ref[...])
    u = dot(t, si)
    out_ref[:h, :h] = ai_ref[...] + dot(u, t, NT)
    out_ref[:h, h:] = -u
    out_ref[h:, :h] = -u.T
    out_ref[h:, h:] = si


def choose_kernel(col_ref, *refs):
    parts, (out_ref, turned_ref) = refs[:8], refs[8:]
    mine = parts[0][...]
    for k in range(1, 8):
        mine = jnp.where(col_ref[0] == k, parts[k][...], mine)
    for k in range(8):
        out_ref[k] = mine
    turned_ref[...] = mine.T


def gram_kernel(panel_ref, out_ref, turned_ref):
    turned = panel_ref[...].T
    gram = dot(turned, panel_ref[...]).reshape(8, 32, B)
    out_ref[:, :32, :] = gram[:, :, :128]
    out_ref[:, 32:, :] = gram[:, :, 128:]
    turned_ref[:256], turned_ref[256:] = split(turned)


def panel_product(turned_ref, right):
    hi, lo = split(right)
    both = lax.dot_general(turned_ref[...], hi, NN, preferred_element_type=F32)
    return both[:256] + (both[256:] + lax.dot_general(turned_ref[:256], lo, NN, preferred_element_type=F32))


def give_kernel(core_ref, turned_ref, matrix_ref, vectors_ref, give_ref, keep_ref):
    step = pl.program_id(0)
    product = panel_product(turned_ref, matrix_ref[...])
    give_ref[2 * step, :256, :] = product[:, :128]
    give_ref[2 * step + 1, :256, :] = product[:, 128:]
    mixing = panel_product(turned_ref, vectors_ref[...])
    for b in range(2):
        first, last = mixing[:128, 128 * b : 128 * b + 128], mixing[128:, 128 * b : 128 * b + 128]
        first, last = first.reshape(8, 16, 128), last.reshape(8, 16, 128)
        place = pl.multiple_of(32 * step + 16 * b, 16)
        keep_ref[:, pl.ds(place, 16), :] = jnp.where(core_ref[0] == 0, first, last)
        give_ref[:, pl.ds(256 + place, 16), :] = jnp.where(core_ref[0] == 0, last, first)


def keep_kernel(core_ref, turned_ref, matrix_ref, keep_ref):
    step = pl.program_id(0)
    product = panel_product(turned_ref, matrix_ref[...])
    keep_ref[2 * step] = product[:, :128]
    keep_ref[2 * step + 1] = product[:, 128:]


def join_kernel(keep_ref, mixing_ref, got_ref, gram_ref, other_ref, out_ref):
    out_ref[:, :256, :] = keep_ref[...] + got_ref[:, :256, :]
    out_ref[:, 256:384, :] = mixing_ref[...] + got_ref[:, 256:, :]
    gram = gram_ref[...] + other_ref[...]
    for m in range(8):
        out_ref[m, 384:, :] = gram


def reduce_kernel(in_ref, turned_ref, product_ref, gram_ref, out_ref):
    own = in_ref[0, :384, :]
    for m in range(1, 8):
        own = own + in_ref[m, :384, :]
    product_ref[...] = own[:256].T
    gram_ref[...] = in_ref[:, 384:, :]
    for m in range(8):
        out_ref[m, :384, :] = own
        out_ref[m, 384:, :] = turned_ref[...]


def coupling_kernel(panel_ref, product_ref, out_ref):
    total = jnp.zeros((B, B), F32)
    for m in range(0, 8, 2):
        left = jnp.concatenate([panel_ref[m], panel_ref[m + 1]], axis=1)
        right = jnp.concatenate([product_ref[m], product_ref[m + 1]], axis=1)
        total = total + dot3(split(left), split(right), NT)
    out_ref[...] = total.reshape(16, 16, B)


def sum_kernel(in_ref, out_ref):
    total = jnp.sum(in_ref[...], axis=0)
    for m in range(out_ref.shape[0]):
        out_ref[m] = total


def scale_kernel(panel_ref, product_ref, inverse_ref, left_ref, out_ref):
    inverse = inverse_ref[...]
    hi, lo = split(2.0 * dot(panel_ref[...], inverse))
    left_ref[:, :256], left_ref[:, 256:512], left_ref[:, 512:] = hi, hi, lo
    for k in range(4):
        out_ref[k] = 2.0 * dot(product_ref[k], inverse)


def rotate_kernel(core_ref, left_ref, mine_ref, other_ref, vectors_ref, out_ref):
    core = core_ref[0]
    mine, other = mine_ref[...], other_ref[...]
    both = jnp.where(core == 0, mine, other), jnp.where(core == 0, other, mine)
    lanes = [jnp.concatenate([h[:, k : k + 16, :].reshape(128, 128) for h in both], axis=0) for k in (0, 16)]
    hi, lo = split(jnp.concatenate(lanes, axis=1))
    right = jnp.concatenate([hi, lo, hi], axis=0)
    out_ref[...] = vectors_ref[...] - lax.dot_general(left_ref[...], right, NN, preferred_element_type=F32)


def update_kernel(
    where_ref, first_ref, near_ref, far_ref, inverse_ref, coupling_ref,
    mine_ref, other_ref, pmine_ref, pother_ref, matrix_ref, out_ref, left_ref, product_ref,
):
    step = pl.program_id(0)

    @pl.when(step == 0)
    def _():
        for k in range(4):
            for piece_ref, zh in ((near_ref, where_ref[2]), (far_ref, 1 - where_ref[2])):
                place = (lax.rem(where_ref[1] + k, 4) * 2 + zh) * 128
                product_ref[pl.ds(pl.multiple_of(place, 128), 128), :] = piece_ref[k]
        small = dot(coupling_ref[...].reshape(B, B), inverse_ref[...])
        hi, lo = split(small)
        right = jnp.concatenate([hi, lo, hi], axis=0)
        u = product_ref[...] - 2.0 * lax.dot_general(first_ref[...], right, NN, preferred_element_type=F32)
        hi, lo = split(u)
        left_ref[:, :768] = first_ref[...]
        left_ref[:, 768:1024], left_ref[:, 1024:1280], left_ref[:, 1280:] = hi, hi, lo

    mine = step // 4 == where_ref[0]
    product = jnp.where(mine, mine_ref[...], other_ref[...])
    panel = jnp.where(mine, pmine_ref[...], pother_ref[...])
    halves = [split(jnp.concatenate([a[0], a[1]], axis=1)) for a in (product, panel)]
    right = jnp.concatenate([x for hi, lo in halves for x in (hi, lo, hi)], axis=0)
    out_ref[...] = matrix_ref[...] - lax.dot_general(left_ref[...], right, NN, preferred_element_type=F32)


def repeat(block, n=8):
    return jnp.broadcast_to(block[None], (n,) + block.shape)


def exchange(blocks, axes):
    return lax.all_to_all(blocks, axes, 0, 0, tiled=True)


def swap_cores(array):
    return lax.ppermute(array, "co", [(0, 1), (1, 0)])


def gather_x(block):
    return jnp.stack([block] + [lax.ppermute(block, "x", [((x + k) % 4, x) for x in range(4)]) for k in (1, 2, 3)])


def flip_pairs():
    pairs = []
    for i in range(16):
        for k in range(8):
            pairs.append((i * 8 + k, (k * 2 + i % 2) * 8 + i // 2))
    return pairs


VMEM = pl.BlockSpec(memory_space=pltpu.VMEM)
SMEM = pl.BlockSpec(memory_space=pltpu.SMEM)


def whole(*shape):
    return pl.BlockSpec(shape, lambda t: (0,) * len(shape))


def body(matrix, vectors):
    rows_here = matrix.shape[0]
    row_index = lax.axis_index(ROW)
    col_index = lax.axis_index(COL)
    core = lax.axis_index("co").astype(jnp.int32).reshape(1)
    where = jnp.stack([core[0], lax.axis_index("x").astype(jnp.int32), lax.axis_index("zh").astype(jnp.int32)])
    there = flip_pairs()
    back = [(b, a) for a, b in there]

    global_rows = row_index * rows_here + jnp.arange(rows_here, dtype=jnp.int32)
    panel = jnp.where(global_rows[:, None] >= B, matrix[:, :B], F32(0.0))
    parts = [panel[:128]]
    for k in range(1, 8):
        parts.append(lax.ppermute(panel[k * 128 : (k + 1) * 128], COL, [(0, k)]))
    sent, turned = call(
        choose_kernel, (f32(8, 128, 256), f32(256, 128)), 1, in_specs=[SMEM] + [VMEM] * 8
    )(col_index.astype(jnp.int32).reshape(1), *parts)
    panel_rows, turned = lax.optimization_barrier((exchange(sent, COL).reshape(1024, B), turned))
    turned = lax.ppermute(turned, ALL, there)
    gram, stacked = call(gram_kernel, (f32(8, 64, 128), jax.ShapeDtypeStruct((512, 1024), BF16)), 2, 12)(panel_rows)
    gram = exchange(gram, CHIPS)
    give, mixing = call(
        give_kernel,
        (f32(8, 384, 128), f32(8, 128, 128)),
        8,
        60,
        grid_spec=pltpu.PrefetchScalarGridSpec(
            num_scalar_prefetch=1,
            grid=(4,),
            in_specs=[
                pl.BlockSpec((512, 1024), lambda t, core: (0, 0)),
                pl.BlockSpec((1024, 256), lambda t, core: (0, (1 - core[0]) * 4 + t)),
                pl.BlockSpec((1024, 256), lambda t, core: (0, t)),
            ],
            out_specs=(
                pl.BlockSpec((8, 384, 128), lambda t, core: (0, 0, 0)),
                pl.BlockSpec((8, 128, 128), lambda t, core: (0, 0, 0)),
            ),
        ),
    )(core, stacked, matrix, vectors)
    give, mixing, turned, gram, stacked = lax.optimization_barrier((give, mixing, turned, gram, stacked))
    gram = jnp.sum(gram, axis=0)
    keep = call(
        keep_kernel,
        f32(8, 256, 128),
        5,
        60,
        grid_spec=pltpu.PrefetchScalarGridSpec(
            num_scalar_prefetch=1,
            grid=(4,),
            in_specs=[
                pl.BlockSpec((512, 1024), lambda t, core: (0, 0)),
                pl.BlockSpec((1024, 256), lambda t, core: (0, core[0] * 4 + t)),
            ],
            out_specs=pl.BlockSpec((8, 256, 128), lambda t, core: (0, 0, 0)),
        ),
    )(core, stacked, matrix)
    got, other_gram, keep = lax.optimization_barrier((swap_cores(give), swap_cores(gram), keep))
    came = exchange(call(join_kernel, f32(8, 448, 128), 1, 12)(keep, mixing, got, gram, other_gram), CHIPS)

    product, gram, sent = call(reduce_kernel, (f32(128, 256), f32(8, 64, 128), f32(8, 640, 128)), 2, 12)(came, turned)
    final = exchange(sent, CHIPS)
    near = gather_x(lax.ppermute(product, ALL, back))
    ai, t, schur = call(invert_first, (f32(128, 128),) * 3, 9)(gram)
    inverse = call(invert_second, f32(B, B), 9)(ai, t, schur)
    first, near = call(
        scale_kernel, (jax.ShapeDtypeStruct((1024, 768), BF16), f32(4, 128, 256)), 4, 20
    )(panel_rows, near, inverse)
    final, near, first, inverse = lax.optimization_barrier((final, near, first, inverse))
    other = swap_cores(final)
    far = lax.ppermute(near, "zh", [(0, 1), (1, 0)])
    coupling = call(
        coupling_kernel,
        f32(16, 16, 256),
        2,
        grid=(1,),
        in_specs=[
            pl.BlockSpec((pl.Element(8), pl.Element(256), pl.Element(128)), lambda t: (0, 384, 0)),
            pl.BlockSpec((8, 256, 128), lambda t: (0, 0, 0)),
        ],
        out_specs=whole(16, 16, 256),
    )(final, final)
    coupling = exchange(coupling, COUPLED)
    mixing = pl.BlockSpec((8, 32, 128), lambda t: (0, 8 + t, 0))
    rotated = call(
        rotate_kernel,
        f32(1024, 1024),
        6,
        60,
        grid=(4,),
        in_specs=[SMEM, whole(1024, 768), mixing, mixing, pl.BlockSpec((1024, 256), lambda t: (0, t))],
        out_specs=pl.BlockSpec((1024, 256), lambda t: (0, t)),
    )(core, first, final, other, vectors)
    coupling, rotated = lax.optimization_barrier((coupling, rotated))
    coupling = exchange(call(sum_kernel, f32(16, 16, 256), 1)(coupling), COUPLED)

    pair = pl.BlockSpec((2, 256, 128), lambda t: (t % 4, 0, 0))
    piece = whole(4, 128, 256)
    panel_pair = pl.BlockSpec((pl.Element(2), pl.Element(256), pl.Element(128)), lambda t: (2 * (t % 4), 384, 0))
    updated = call(
        update_kernel,
        f32(1024, 2048),
        12,
        60,
        grid=(8,),
        in_specs=[
            SMEM, whole(1024, 768), piece, piece, whole(256, 256), whole(16, 16, 256), pair, pair, panel_pair,
            panel_pair, pl.BlockSpec((1024, 256), lambda t: (0, t)),
        ],
        out_specs=pl.BlockSpec((1024, 256), lambda t: (0, t)),
        scratch_shapes=[pltpu.VMEM((1024, 1536), BF16), pltpu.VMEM((1024, 256), F32)],
    )(where, first, near, far, inverse, coupling, final, other, final, other, matrix)
    return (updated, rotated)


def solution(mesh):
    fine = Mesh(mesh.devices.reshape(4, 2, 2, 4, 2), ALL)
    placed = (P(ROW, COL), P(ROW, COL))
    return jax.shard_map(body, mesh=fine, in_specs=placed, out_specs=placed, check_vma=False)
```

```python
import jax
import jax.numpy as jnp
from jax import lax
from jax.experimental import pallas as pl
from jax.experimental.pallas import tpu as pltpu
from jax.sharding import Mesh
from jax.sharding import PartitionSpec as P

B = 256
ROW = ("y", "zl", "co")
CHIPS = ("y", "zl")
COL = ("x", "zh")
COUPLED = ("co", "x", "zh")
ALL = ("y", "zl", "co", "x", "zh")
HIGHEST = lax.Precision.HIGHEST
F32 = jnp.float32
BF16 = jnp.bfloat16
NN = (((1,), (0,)), ((), ()))
NT = (((1,), (1,)), ((), ()))
TN = (((0,), (0,)), ((), ()))


def dot(left, right, dims=NN):
    return lax.dot_general(left, right, dims, preferred_element_type=F32, precision=HIGHEST)


def split(x):
    hi = x.astype(BF16)
    return hi, (x - hi.astype(F32)).astype(BF16)


def dot3(left, right, dims=NN):
    (ah, al), (bh, bl) = left, right
    f = lambda a, b: lax.dot_general(a, b, dims, preferred_element_type=F32)
    return f(ah, bh) + (f(ah, bl) + f(al, bh))


def call(kernel, out_shape, us, mib=8, **kw):
    cost = pl.CostEstimate(flops=int(us * 1e9), bytes_accessed=1024, transcendentals=0)
    params = pltpu.CompilerParams(vmem_limit_bytes=mib * 1024 * 1024)
    return pl.pallas_call(kernel, out_shape=out_shape, cost_estimate=cost, compiler_params=params, **kw)


def f32(*shape):
    return jax.ShapeDtypeStruct(shape, F32)


def sweep_all(block):
    n, group = 128, 16
    lane = lax.broadcasted_iota(jnp.int32, (8, n), 1)
    line = lax.broadcasted_iota(jnp.int32, (8, n), 0)
    tiles = n // 8

    def step(_, s):
        s = list(s)
        for k in range(0, group, 2):
            t, sub = k // 8, k % 8
            r0 = jnp.broadcast_to(s[t][sub : sub + 1, :], (8, n))
            r1 = jnp.broadcast_to(s[t][sub + 1 : sub + 2, :], (8, n))
            a = jnp.broadcast_to(r0[:, k : k + 1], (8, n))
            b = jnp.broadcast_to(r1[:, k : k + 1], (8, n))
            d = jnp.broadcast_to(r1[:, k + 1 : k + 2], (8, n))
            scale = 1.0 / (a * d - b * b)
            ia, ib, ic = d * scale, -b * scale, a * scale
            q0 = jnp.where(lane == k, -ia, jnp.where(lane == k + 1, -ib, ia * r0 + ib * r1))
            q1 = jnp.where(lane == k, -ib, jnp.where(lane == k + 1, -ic, ib * r0 + ic * r1))
            pivots = (lane == k) | (lane == k + 1)
            for u in range(tiles):
                c0 = jnp.broadcast_to(s[u][:, k : k + 1], (8, n))
                c1 = jnp.broadcast_to(s[u][:, k + 1 : k + 2], (8, n))
                new = jnp.where(pivots, 0.0, s[u]) - c0 * q0 - c1 * q1
                if u == t:
                    new = jnp.where(line == sub, q0, jnp.where(line == sub + 1, q1, new))
                s[u] = new
        s = s[group // 8 :] + s[: group // 8]
        return tuple(pltpu.roll(v, n - group, 1) for v in s)

    out = lax.fori_loop(0, n // group, step, tuple(block[8 * u : 8 * u + 8, :] for u in range(tiles)))
    return jnp.concatenate(out, axis=0)


def invert_first(gram_ref, ai_ref, t_ref, schur_ref):
    def part(lo, lanes):
        return jnp.concatenate([gram_ref[m, 32 * lanes : 32 * lanes + 32, :] for m in range(lo, lo + 4)], axis=0)

    b = part(0, 1)
    ai = -sweep_all(part(0, 0))
    t = dot(ai, b)
    ai_ref[...] = ai
    t_ref[...] = t
    schur_ref[...] = part(4, 1) - dot(b, t, TN)


def invert_second(ai_ref, t_ref, schur_ref, out_ref):
    h = B // 2
    t = t_ref[...]
    si = -sweep_all(schur_ref[...])
    u = dot(t, si)
    out_ref[:h, :h] = ai_ref[...] + dot(u, t, NT)
    out_ref[:h, h:] = -u
    out_ref[h:, :h] = -u.T
    out_ref[h:, h:] = si


def choose_kernel(col_ref, *refs):
    parts, (out_ref, turned_ref) = refs[:8], refs[8:]
    mine = parts[0][...]
    for k in range(1, 8):
        mine = jnp.where(col_ref[0] == k, parts[k][...], mine)
    for k in range(8):
        out_ref[k] = mine
    turned_ref[...] = mine.T


def gram_kernel(panel_ref, block_ref, out_ref, turned_ref):
    turned = panel_ref[...].T
    gram = dot(turned, panel_ref[...]).reshape(8, 32, B)
    for m in range(8):
        out_ref[m, :256, :] = block_ref[...]
    out_ref[:, 256:288, :] = gram[:, :, :128]
    out_ref[:, 288:, :] = gram[:, :, 128:]
    turned_ref[:256], turned_ref[256:] = split(turned)


def panel_product(turned_ref, right):
    hi, lo = split(right)
    both = lax.dot_general(turned_ref[...], hi, NN, preferred_element_type=F32)
    return both[:256] + (both[256:] + lax.dot_general(turned_ref[:256], lo, NN, preferred_element_type=F32))


def product_kernel(core_ref, turned_ref, theirs_ref, mine_ref, vectors_ref, give_ref, keep_ref):
    step = pl.program_id(0)
    for matrix_ref, out_ref in ((theirs_ref, give_ref), (mine_ref, keep_ref)):
        product = panel_product(turned_ref, matrix_ref[...])
        out_ref[2 * step, :256, :] = product[:, :128]
        out_ref[2 * step + 1, :256, :] = product[:, 128:]
    mixing = panel_product(turned_ref, vectors_ref[...])
    for b in range(2):
        first, last = mixing[:128, 128 * b : 128 * b + 128], mixing[128:, 128 * b : 128 * b + 128]
        first, last = first.reshape(8, 16, 128), last.reshape(8, 16, 128)
        place = pl.multiple_of(32 * step + 16 * b, 16)
        keep_ref[:, pl.ds(256 + place, 16), :] = jnp.where(core_ref[0] == 0, first, last)
        give_ref[:, pl.ds(256 + place, 16), :] = jnp.where(core_ref[0] == 0, last, first)


def join_kernel(keep_ref, got_ref, gram_ref, other_ref, out_ref):
    out_ref[:, :384, :] = keep_ref[...] + got_ref[...]
    gram = gram_ref[...] + other_ref[...]
    for m in range(8):
        out_ref[m, 384:, :] = gram


def reduce_kernel(in_ref, product_ref, gram_ref, out_ref):
    own = in_ref[0, :384, :]
    for m in range(1, 8):
        own = own + in_ref[m, :384, :]
    product_ref[...] = own[:256].T
    gram_ref[...] = in_ref[:, 384:, :]
    for m in range(8):
        out_ref[m] = own


def coupling_kernel(panel_ref, product_ref, out_ref):
    total = jnp.zeros((B, B), F32)
    for m in range(0, 8, 2):
        left = jnp.concatenate([panel_ref[m], panel_ref[m + 1]], axis=1)
        right = jnp.concatenate([product_ref[m], product_ref[m + 1]], axis=1)
        total = total + dot3(split(left), split(right), NT)
    out_ref[...] = total.reshape(16, 16, B)


def sum_kernel(in_ref, out_ref):
    total = jnp.sum(in_ref[...], axis=0)
    for m in range(out_ref.shape[0]):
        out_ref[m] = total


def scale_kernel(panel_ref, product_ref, inverse_ref, left_ref, out_ref):
    inverse = inverse_ref[...]
    hi, lo = split(2.0 * dot(panel_ref[...], inverse))
    left_ref[:, :256], left_ref[:, 256:512], left_ref[:, 512:] = hi, hi, lo
    for k in range(4):
        out_ref[k] = 2.0 * dot(product_ref[k], inverse)


def rotate_kernel(core_ref, left_ref, mine_ref, other_ref, vectors_ref, out_ref):
    core = core_ref[0]
    mine, other = mine_ref[...], other_ref[...]
    both = jnp.where(core == 0, mine, other), jnp.where(core == 0, other, mine)
    lanes = [jnp.concatenate([h[:, k : k + 16, :].reshape(128, 128) for h in both], axis=0) for k in (0, 16)]
    hi, lo = split(jnp.concatenate(lanes, axis=1))
    right = jnp.concatenate([hi, lo, hi], axis=0)
    out_ref[...] = vectors_ref[...] - lax.dot_general(left_ref[...], right, NN, preferred_element_type=F32)


def update_kernel(
    where_ref, first_ref, near_ref, far_ref, inverse_ref, coupling_ref,
    mine_ref, other_ref, pmine_ref, pother_ref, matrix_ref, out_ref, left_ref, product_ref,
):
    step = pl.program_id(0)

    @pl.when(step == 0)
    def _():
        for k in range(4):
            for piece_ref, zh in ((near_ref, where_ref[2]), (far_ref, 1 - where_ref[2])):
                place = (lax.rem(where_ref[1] + k, 4) * 2 + zh) * 128
                product_ref[pl.ds(pl.multiple_of(place, 128), 128), :] = piece_ref[k]
        small = dot(coupling_ref[...].reshape(B, B), inverse_ref[...])
        hi, lo = split(small)
        right = jnp.concatenate([hi, lo, hi], axis=0)
        u = product_ref[...] - 2.0 * lax.dot_general(first_ref[...], right, NN, preferred_element_type=F32)
        hi, lo = split(u)
        left_ref[:, :768] = first_ref[...]
        left_ref[:, 768:1024], left_ref[:, 1024:1280], left_ref[:, 1280:] = hi, hi, lo

    mine = step // 4 == where_ref[0]
    product = jnp.where(mine, mine_ref[...], other_ref[...])
    panel = jnp.where(mine, pmine_ref[...], pother_ref[...])
    halves = [split(jnp.concatenate([a[0], a[1]], axis=1)) for a in (product, panel)]
    right = jnp.concatenate([x for hi, lo in halves for x in (hi, lo, hi)], axis=0)
    out_ref[...] = matrix_ref[...] - lax.dot_general(left_ref[...], right, NN, preferred_element_type=F32)


def repeat(block, n=8):
    return jnp.broadcast_to(block[None], (n,) + block.shape)


def exchange(blocks, axes):
    return lax.all_to_all(blocks, axes, 0, 0, tiled=True)


def swap_cores(array):
    return lax.ppermute(array, "co", [(0, 1), (1, 0)])


def gather_x(block):
    return jnp.stack([block] + [lax.ppermute(block, "x", [((x + k) % 4, x) for x in range(4)]) for k in (1, 2, 3)])


def flip_pairs():
    pairs = []
    for i in range(16):
        for k in range(8):
            pairs.append((i * 8 + k, (k * 2 + i % 2) * 8 + i // 2))
    return pairs


VMEM = pl.BlockSpec(memory_space=pltpu.VMEM)
SMEM = pl.BlockSpec(memory_space=pltpu.SMEM)


def whole(*shape):
    return pl.BlockSpec(shape, lambda t: (0,) * len(shape))


def fixed(*shape):
    return pl.BlockSpec(shape, lambda t, w: (0,) * len(shape))


def body(matrix, vectors):
    rows_here = matrix.shape[0]
    row_index = lax.axis_index(ROW)
    col_index = lax.axis_index(COL)
    core = lax.axis_index("co").astype(jnp.int32).reshape(1)
    where = jnp.stack([core[0], lax.axis_index("x").astype(jnp.int32), lax.axis_index("zh").astype(jnp.int32)])
    there = flip_pairs()
    back = [(b, a) for a, b in there]

    global_rows = row_index * rows_here + jnp.arange(rows_here, dtype=jnp.int32)
    columns = jnp.where(global_rows[:, None] >= B, matrix[:, :B], F32(0.0))
    parts = [columns[:128]]
    for k in range(1, 8):
        parts.append(lax.ppermute(columns[k * 128 : (k + 1) * 128], COL, [(0, k)]))
    sent, turned = call(
        choose_kernel, (f32(8, 128, 256), f32(256, 128)), 1, in_specs=[SMEM] + [VMEM] * 8
    )(col_index.astype(jnp.int32).reshape(1), *parts)
    turned = lax.ppermute(turned, ALL, there)
    panel_rows = exchange(sent, COL).reshape(1024, B)
    sent, stacked = call(gram_kernel, (f32(8, 320, 128), jax.ShapeDtypeStruct((512, 1024), BF16)), 2, 12)(
        panel_rows, turned
    )
    panel = exchange(sent, CHIPS)
    half = pl.BlockSpec((8, 384, 128), lambda t, core: (0, 0, 0))
    give, keep = call(
        product_kernel,
        (f32(8, 384, 128), f32(8, 384, 128)),
        12,
        60,
        grid_spec=pltpu.PrefetchScalarGridSpec(
            num_scalar_prefetch=1,
            grid=(4,),
            in_specs=[
                pl.BlockSpec((512, 1024), lambda t, core: (0, 0)),
                pl.BlockSpec((1024, 256), lambda t, core: (0, (1 - core[0]) * 4 + t)),
                pl.BlockSpec((1024, 256), lambda t, core: (0, core[0] * 4 + t)),
                pl.BlockSpec((1024, 256), lambda t, core: (0, t)),
            ],
            out_specs=(half, half),
        ),
    )(core, stacked, matrix, matrix, vectors)
    give, keep, panel = lax.optimization_barrier((give, keep, panel))
    got = swap_cores(give)
    gram = jnp.sum(panel[:, 256:], axis=0)
    other_gram = swap_cores(gram)
    other_panel = swap_cores(panel)
    came = exchange(call(join_kernel, f32(8, 448, 128), 1, 12)(keep, got, gram, other_gram), CHIPS)

    product, gram, sent = call(reduce_kernel, (f32(128, 256), f32(8, 64, 128), f32(8, 384, 128)), 2, 12)(came)
    final = exchange(sent, CHIPS)
    near = gather_x(lax.ppermute(product, ALL, back))
    ai, t, schur = call(invert_first, (f32(128, 128),) * 3, 9)(gram)
    inverse = call(invert_second, f32(B, B), 9)(ai, t, schur)
    first, near = call(
        scale_kernel, (jax.ShapeDtypeStruct((1024, 768), BF16), f32(4, 128, 256)), 4, 20
    )(panel_rows, near, inverse)
    final, near, first, inverse = lax.optimization_barrier((final, near, first, inverse))
    other = swap_cores(final)
    far = lax.ppermute(near, "zh", [(0, 1), (1, 0)])
    coupling = call(
        coupling_kernel,
        f32(16, 16, 256),
        2,
        grid=(1,),
        in_specs=[
            pl.BlockSpec((8, 256, 128), lambda t: (0, 0, 0)),
            pl.BlockSpec((8, 256, 128), lambda t: (0, 0, 0)),
        ],
        out_specs=whole(16, 16, 256),
    )(panel, final)
    coupling = exchange(coupling, COUPLED)
    mixing = pl.BlockSpec((8, 32, 128), lambda t: (0, 8 + t, 0))
    rotated = call(
        rotate_kernel,
        f32(1024, 1024),
        6,
        60,
        grid=(4,),
        in_specs=[SMEM, whole(1024, 768), mixing, mixing, pl.BlockSpec((1024, 256), lambda t: (0, t))],
        out_specs=pl.BlockSpec((1024, 256), lambda t: (0, t)),
    )(core, first, final, other, vectors)
    coupling, rotated = lax.optimization_barrier((coupling, rotated))
    coupling = exchange(call(sum_kernel, f32(16, 16, 256), 1)(coupling), COUPLED)

    mine = pl.BlockSpec((2, 256, 128), lambda t, w: (jnp.clip(t - 4 * w[0], 0, 3), 0, 0))
    theirs = pl.BlockSpec((2, 256, 128), lambda t, w: (jnp.clip(t - 4 * (1 - w[0]), 0, 3), 0, 0))
    piece = fixed(4, 128, 256)
    updated = call(
        update_kernel,
        f32(1024, 2048),
        12,
        60,
        grid_spec=pltpu.PrefetchScalarGridSpec(
            num_scalar_prefetch=1,
            grid=(8,),
            in_specs=[
                fixed(1024, 768), piece, piece, fixed(256, 256), fixed(16, 16, 256), mine, theirs, mine, theirs,
                pl.BlockSpec((1024, 256), lambda t, w: (0, t)),
            ],
            out_specs=pl.BlockSpec((1024, 256), lambda t, w: (0, t)),
            scratch_shapes=[pltpu.VMEM((1024, 1536), BF16), pltpu.VMEM((1024, 256), F32)],
        ),
    )(where, first, near, far, inverse, coupling, final, other, panel, other_panel, matrix)
    return (updated, rotated)


def solution(mesh):
    fine = Mesh(mesh.devices.reshape(4, 2, 2, 4, 2), ALL)
    placed = (P(ROW, COL), P(ROW, COL))
    return jax.shard_map(body, mesh=fine, in_specs=placed, out_specs=placed, check_vma=False)
```

```python
import jax
import jax.numpy as jnp
from jax import lax
from jax.experimental import pallas as pl
from jax.experimental.pallas import tpu as pltpu
from jax.sharding import Mesh
from jax.sharding import PartitionSpec as P

B = 256
ROW = ("y", "zl", "co")
CHIPS = ("y", "zl")
COL = ("x", "zh")
COUPLED = ("co", "x", "zh")
ALL = ("y", "zl", "co", "x", "zh")
HIGHEST = lax.Precision.HIGHEST
F32 = jnp.float32
BF16 = jnp.bfloat16
NN = (((1,), (0,)), ((), ()))
NT = (((1,), (1,)), ((), ()))
TN = (((0,), (0,)), ((), ()))


def dot(left, right, dims=NN):
    return lax.dot_general(left, right, dims, preferred_element_type=F32, precision=HIGHEST)


def split(x):
    hi = x.astype(BF16)
    return hi, (x - hi.astype(F32)).astype(BF16)


def dot3(left, right, dims=NN):
    (ah, al), (bh, bl) = left, right
    f = lambda a, b: lax.dot_general(a, b, dims, preferred_element_type=F32)
    return f(ah, bh) + (f(ah, bl) + f(al, bh))


def call(kernel, out_shape, us, mib=8, **kw):
    cost = pl.CostEstimate(flops=int(us * 1e9), bytes_accessed=1024, transcendentals=0)
    params = pltpu.CompilerParams(vmem_limit_bytes=mib * 1024 * 1024)
    return pl.pallas_call(kernel, out_shape=out_shape, cost_estimate=cost, compiler_params=params, **kw)


def f32(*shape):
    return jax.ShapeDtypeStruct(shape, F32)


def invert2(a, b, d):
    scale = 1.0 / (a * d - b * b)
    return d * scale, -(b * scale), a * scale


def invert4(d):
    a00, a01, a11 = invert2(d[0][0], d[0][1], d[1][1])
    a = ((a00, a01), (a01, a11))
    t = [[a[i][0] * d[0][j] + a[i][1] * d[1][j] for j in (2, 3)] for i in (0, 1)]
    s = lambda i, j: d[i][j] - (d[0][i] * t[0][j - 2] + d[1][i] * t[1][j - 2])
    s00, s01, s11 = invert2(s(2, 2), s(2, 3), s(3, 3))
    c = ((s00, s01), (s01, s11))
    u = [[t[i][0] * c[0][j] + t[i][1] * c[1][j] for j in (0, 1)] for i in (0, 1)]
    top = [[a[i][j] + (u[i][0] * t[j][0] + u[i][1] * t[j][1]) for j in (0, 1)] for i in (0, 1)]
    top[1][0] = top[0][1]
    return [
        [top[0][0], top[0][1], -u[0][0], -u[0][1]],
        [top[1][0], top[1][1], -u[1][0], -u[1][1]],
        [-u[0][0], -u[1][0], s00, s01],
        [-u[0][1], -u[1][1], s01, s11],
    ]


def sweep_all(block):
    n, group, size = 128, 16, 4
    lane = lax.broadcasted_iota(jnp.int32, (8, n), 1)
    line = lax.broadcasted_iota(jnp.int32, (8, n), 0)
    tiles = n // 8

    def column(tile, k):
        return jnp.broadcast_to(tile[:, k : k + 1], (8, n))

    def step(_, s):
        s = list(s)
        for k in range(0, group, size):
            own, sub = k // 8, k % 8
            rows = [jnp.broadcast_to(s[own][sub + i : sub + i + 1, :], (8, n)) for i in range(size)]
            d = [[column(rows[i], k + j) if j >= i else None for j in range(size)] for i in range(size)]
            inverse = invert4(d)
            scaled = []
            for i in range(size):
                e = inverse[i]
                q = (e[0] * rows[0] + e[1] * rows[1]) + (e[2] * rows[2] + e[3] * rows[3])
                for j in range(size):
                    q = jnp.where(lane == k + j, -e[j], q)
                scaled.append(q)
            pivots = (lane >= k) & (lane < k + size)
            for u in range(tiles):
                c = [column(s[u], k + i) for i in range(size)]
                change = (c[0] * scaled[0] + c[1] * scaled[1]) + (c[2] * scaled[2] + c[3] * scaled[3])
                new = jnp.where(pivots, 0.0, s[u]) - change
                if u == own:
                    for i in range(size):
                        new = jnp.where(line == sub + i, scaled[i], new)
                s[u] = new
        s = s[group // 8 :] + s[: group // 8]
        return tuple(pltpu.roll(v, n - group, 1) for v in s)

    out = lax.fori_loop(0, n // group, step, tuple(block[8 * u : 8 * u + 8, :] for u in range(tiles)))
    return jnp.concatenate(out, axis=0)


def invert_first(gram_ref, ai_ref, t_ref, schur_ref):
    def part(lo, lanes):
        return jnp.concatenate([gram_ref[m, 32 * lanes : 32 * lanes + 32, :] for m in range(lo, lo + 4)], axis=0)

    b = part(0, 1)
    ai = -sweep_all(part(0, 0))
    t = dot(ai, b)
    ai_ref[...] = ai
    t_ref[...] = t
    schur_ref[...] = part(4, 1) - dot(b, t, TN)


def invert_second(ai_ref, t_ref, schur_ref, out_ref):
    h = B // 2
    t = t_ref[...]
    si = -sweep_all(schur_ref[...])
    u = dot(t, si)
    out_ref[:h, :h] = ai_ref[...] + dot(u, t, NT)
    out_ref[:h, h:] = -u
    out_ref[h:, :h] = -u.T
    out_ref[h:, h:] = si


def choose_kernel(col_ref, *refs):
    parts, (out_ref, turned_ref) = refs[:8], refs[8:]
    mine = parts[0][...]
    for k in range(1, 8):
        mine = jnp.where(col_ref[0] == k, parts[k][...], mine)
    for k in range(8):
        out_ref[k] = mine
    turned_ref[...] = mine.T


def gram_kernel(panel_ref, block_ref, out_ref, turned_ref):
    turned = panel_ref[...].T
    gram = dot(turned, panel_ref[...]).reshape(8, 32, B)
    for m in range(8):
        out_ref[m, :256, :] = block_ref[...]
    out_ref[:, 256:288, :] = gram[:, :, :128]
    out_ref[:, 288:, :] = gram[:, :, 128:]
    turned_ref[:256], turned_ref[256:] = split(turned)


def panel_product(turned_ref, right):
    hi, lo = split(right)
    both = lax.dot_general(turned_ref[...], hi, NN, preferred_element_type=F32)
    return both[:256] + (both[256:] + lax.dot_general(turned_ref[:256], lo, NN, preferred_element_type=F32))


def product_kernel(core_ref, turned_ref, theirs_ref, mine_ref, vectors_ref, give_ref, keep_ref):
    step = pl.program_id(0)
    for matrix_ref, out_ref in ((theirs_ref, give_ref), (mine_ref, keep_ref)):
        product = panel_product(turned_ref, matrix_ref[...])
        out_ref[2 * step, :256, :] = product[:, :128]
        out_ref[2 * step + 1, :256, :] = product[:, 128:]
    mixing = panel_product(turned_ref, vectors_ref[...])
    for b in range(2):
        first, last = mixing[:128, 128 * b : 128 * b + 128], mixing[128:, 128 * b : 128 * b + 128]
        first, last = first.reshape(8, 16, 128), last.reshape(8, 16, 128)
        place = pl.multiple_of(32 * step + 16 * b, 16)
        keep_ref[:, pl.ds(256 + place, 16), :] = jnp.where(core_ref[0] == 0, first, last)
        give_ref[:, pl.ds(256 + place, 16), :] = jnp.where(core_ref[0] == 0, last, first)


def join_kernel(keep_ref, got_ref, gram_ref, other_ref, out_ref):
    out_ref[:, :384, :] = keep_ref[...] + got_ref[...]
    gram = gram_ref[...] + other_ref[...]
    for m in range(8):
        out_ref[m, 384:, :] = gram


def reduce_kernel(in_ref, product_ref, own_ref, gram_ref):
    own = in_ref[0, :384, :]
    for m in range(1, 8):
        own = own + in_ref[m, :384, :]
    product_ref[...] = own[:256].T
    own_ref[...] = own
    gram_ref[...] = in_ref[:, 384:, :]


def coupling_kernel(panel_ref, product_ref, out_ref):
    total = jnp.zeros((B, B), F32)
    for m in range(0, 8, 2):
        left = jnp.concatenate([panel_ref[m], panel_ref[m + 1]], axis=1)
        right = jnp.concatenate([product_ref[m], product_ref[m + 1]], axis=1)
        total = total + dot3(split(left), split(right), NT)
    out_ref[...] = total.reshape(16, 16, B)


def sum_kernel(in_ref, out_ref):
    total = jnp.sum(in_ref[...], axis=0)
    for m in range(out_ref.shape[0]):
        out_ref[m] = total


def scale_kernel(panel_ref, product_ref, inverse_ref, left_ref, out_ref):
    inverse = inverse_ref[...]
    hi, lo = split(2.0 * dot(panel_ref[...], inverse))
    left_ref[:, :256], left_ref[:, 256:512], left_ref[:, 512:] = hi, hi, lo
    for k in range(4):
        out_ref[k] = 2.0 * dot(product_ref[k], inverse)


def rotate_kernel(core_ref, left_ref, mine_ref, other_ref, vectors_ref, out_ref):
    core = core_ref[0]
    mine, other = mine_ref[...], other_ref[...]
    both = jnp.where(core == 0, mine, other), jnp.where(core == 0, other, mine)
    lanes = [jnp.concatenate([h[:, k : k + 16, :].reshape(128, 128) for h in both], axis=0) for k in (0, 16)]
    hi, lo = split(jnp.concatenate(lanes, axis=1))
    right = jnp.concatenate([hi, lo, hi], axis=0)
    out_ref[...] = vectors_ref[...] - lax.dot_general(left_ref[...], right, NN, preferred_element_type=F32)


def update_kernel(
    where_ref, first_ref, near_ref, far_ref, inverse_ref, coupling_ref,
    mine_ref, other_ref, pmine_ref, pother_ref, matrix_ref, out_ref, left_ref, product_ref,
):
    step = pl.program_id(0)

    @pl.when(step == 0)
    def _():
        for k in range(4):
            for piece_ref, zh in ((near_ref, where_ref[2]), (far_ref, 1 - where_ref[2])):
                place = (lax.rem(where_ref[1] + k, 4) * 2 + zh) * 128
                product_ref[pl.ds(pl.multiple_of(place, 128), 128), :] = piece_ref[k]
        small = dot(coupling_ref[...].reshape(B, B), inverse_ref[...])
        hi, lo = split(small)
        right = jnp.concatenate([hi, lo, hi], axis=0)
        u = product_ref[...] - 2.0 * lax.dot_general(first_ref[...], right, NN, preferred_element_type=F32)
        hi, lo = split(u)
        left_ref[:, :768] = first_ref[...]
        left_ref[:, 768:1024], left_ref[:, 1024:1280], left_ref[:, 1280:] = hi, hi, lo

    mine = step // 2 == where_ref[0]
    product = jnp.where(mine, mine_ref[...], other_ref[...])
    panel = jnp.where(mine, pmine_ref[...], pother_ref[...])
    halves = [split(jnp.concatenate([a[m] for m in range(4)], axis=1)) for a in (product, panel)]
    right = jnp.concatenate([x for hi, lo in halves for x in (hi, lo, hi)], axis=0)
    out_ref[...] = matrix_ref[...] - lax.dot_general(left_ref[...], right, NN, preferred_element_type=F32)


def repeat(block, n=8):
    return jnp.broadcast_to(block[None], (n,) + block.shape)


def exchange(blocks, axes):
    return lax.all_to_all(blocks, axes, 0, 0, tiled=True)


def swap_cores(array):
    return lax.ppermute(array, "co", [(0, 1), (1, 0)])


def gather_x(block):
    return jnp.stack([block] + [lax.ppermute(block, "x", [((x + k) % 4, x) for x in range(4)]) for k in (1, 2, 3)])


def flip_pairs():
    pairs = []
    for i in range(16):
        for k in range(8):
            pairs.append((i * 8 + k, (k * 2 + i % 2) * 8 + i // 2))
    return pairs


VMEM = pl.BlockSpec(memory_space=pltpu.VMEM)
SMEM = pl.BlockSpec(memory_space=pltpu.SMEM)


def whole(*shape):
    return pl.BlockSpec(shape, lambda t: (0,) * len(shape))


def fixed(*shape):
    return pl.BlockSpec(shape, lambda t, w: (0,) * len(shape))


def body(matrix, vectors):
    rows_here = matrix.shape[0]
    row_index = lax.axis_index(ROW)
    col_index = lax.axis_index(COL)
    core = lax.axis_index("co").astype(jnp.int32).reshape(1)
    where = jnp.stack([core[0], lax.axis_index("x").astype(jnp.int32), lax.axis_index("zh").astype(jnp.int32)])
    there = flip_pairs()
    back = [(b, a) for a, b in there]

    global_rows = row_index * rows_here + jnp.arange(rows_here, dtype=jnp.int32)
    columns = jnp.where(global_rows[:, None] >= B, matrix[:, :B], F32(0.0))
    parts = [columns[:128]]
    for k in range(1, 8):
        parts.append(lax.ppermute(columns[k * 128 : (k + 1) * 128], COL, [(0, k)]))
    sent, turned = call(
        choose_kernel, (f32(8, 128, 256), f32(256, 128)), 1, in_specs=[SMEM] + [VMEM] * 8
    )(col_index.astype(jnp.int32).reshape(1), *parts)
    turned = lax.ppermute(turned, ALL, there)
    panel_rows = exchange(sent, COL).reshape(1024, B)
    sent, stacked = call(gram_kernel, (f32(8, 320, 128), jax.ShapeDtypeStruct((512, 1024), BF16)), 2, 12)(
        panel_rows, turned
    )
    panel = exchange(sent, CHIPS)
    half = pl.BlockSpec((8, 384, 128), lambda t, core: (0, 0, 0))
    give, keep = call(
        product_kernel,
        (f32(8, 384, 128), f32(8, 384, 128)),
        12,
        60,
        grid_spec=pltpu.PrefetchScalarGridSpec(
            num_scalar_prefetch=1,
            grid=(4,),
            in_specs=[
                pl.BlockSpec((512, 1024), lambda t, core: (0, 0)),
                pl.BlockSpec((1024, 256), lambda t, core: (0, (1 - core[0]) * 4 + t)),
                pl.BlockSpec((1024, 256), lambda t, core: (0, core[0] * 4 + t)),
                pl.BlockSpec((1024, 256), lambda t, core: (0, t)),
            ],
            out_specs=(half, half),
        ),
    )(core, stacked, matrix, matrix, vectors)
    give, keep, panel = lax.optimization_barrier((give, keep, panel))
    got = swap_cores(give)
    gram = jnp.sum(panel[:, 256:], axis=0)
    other_gram = swap_cores(gram)
    other_panel = swap_cores(panel)
    came = exchange(call(join_kernel, f32(8, 448, 128), 1, 12)(keep, got, gram, other_gram), CHIPS)

    product, own, gram = call(reduce_kernel, (f32(128, 256), f32(384, 128), f32(8, 64, 128)), 2, 12)(came)
    final = exchange(repeat(own), CHIPS)
    near = gather_x(lax.ppermute(product, ALL, back))
    ai, t, schur = call(invert_first, (f32(128, 128),) * 3, 9)(gram)
    inverse = call(invert_second, f32(B, B), 9)(ai, t, schur)
    first, near = call(
        scale_kernel, (jax.ShapeDtypeStruct((1024, 768), BF16), f32(4, 128, 256)), 4, 20
    )(panel_rows, near, inverse)
    final, near, first, inverse = lax.optimization_barrier((final, near, first, inverse))
    other = swap_cores(final)
    far = lax.ppermute(near, "zh", [(0, 1), (1, 0)])
    coupling = call(
        coupling_kernel,
        f32(16, 16, 256),
        2,
        grid=(1,),
        in_specs=[
            pl.BlockSpec((8, 256, 128), lambda t: (0, 0, 0)),
            pl.BlockSpec((8, 256, 128), lambda t: (0, 0, 0)),
        ],
        out_specs=whole(16, 16, 256),
    )(panel, final)
    coupling = exchange(call(sum_kernel, f32(16, 16, 256), 1)(exchange(coupling, COUPLED)), COUPLED)
    mixing = pl.BlockSpec((8, 32, 128), lambda t: (0, 8 + t, 0))
    rotated = call(
        rotate_kernel,
        f32(1024, 1024),
        6,
        60,
        grid=(4,),
        in_specs=[SMEM, whole(1024, 768), mixing, mixing, pl.BlockSpec((1024, 256), lambda t: (0, t))],
        out_specs=pl.BlockSpec((1024, 256), lambda t: (0, t)),
    )(core, first, final, other, vectors)
    coupling, rotated = lax.optimization_barrier((coupling, rotated))

    mine = pl.BlockSpec((4, 256, 128), lambda t, w: (jnp.clip(t - 2 * w[0], 0, 1), 0, 0))
    theirs = pl.BlockSpec((4, 256, 128), lambda t, w: (jnp.clip(t - 2 * (1 - w[0]), 0, 1), 0, 0))
    piece = fixed(4, 128, 256)
    updated = call(
        update_kernel,
        f32(1024, 2048),
        12,
        60,
        grid_spec=pltpu.PrefetchScalarGridSpec(
            num_scalar_prefetch=1,
            grid=(4,),
            in_specs=[
                fixed(1024, 768), piece, piece, fixed(256, 256), fixed(16, 16, 256), mine, theirs, mine, theirs,
                pl.BlockSpec((1024, 512), lambda t, w: (0, t)),
            ],
            out_specs=pl.BlockSpec((1024, 512), lambda t, w: (0, t)),
            scratch_shapes=[pltpu.VMEM((1024, 1536), BF16), pltpu.VMEM((1024, 256), F32)],
        ),
    )(where, first, near, far, inverse, coupling, final, other, panel, other_panel, matrix)
    return (updated, rotated)


def solution(mesh):
    fine = Mesh(mesh.devices.reshape(4, 2, 2, 4, 2), ALL)
    placed = (P(ROW, COL), P(ROW, COL))
    return jax.shard_map(body, mesh=fine, in_specs=placed, out_specs=placed, check_vma=False)
```

```python
import jax
import jax.numpy as jnp
from jax import lax
from jax.experimental import pallas as pl
from jax.experimental.pallas import tpu as pltpu
from jax.sharding import Mesh
from jax.sharding import PartitionSpec as P

B = 256
ROW = ("y", "zl", "co")
CHIPS = ("y", "zl")
COL = ("x", "zh")
COUPLED = ("co", "x", "zh")
ALL = ("y", "zl", "co", "x", "zh")
HIGHEST = lax.Precision.HIGHEST
F32 = jnp.float32
BF16 = jnp.bfloat16
NN = (((1,), (0,)), ((), ()))
NT = (((1,), (1,)), ((), ()))
TN = (((0,), (0,)), ((), ()))


def dot(left, right, dims=NN):
    return lax.dot_general(left, right, dims, preferred_element_type=F32, precision=HIGHEST)


def split(x):
    hi = x.astype(BF16)
    return hi, (x - hi.astype(F32)).astype(BF16)


def dot3(left, right, dims=NN):
    (ah, al), (bh, bl) = left, right
    f = lambda a, b: lax.dot_general(a, b, dims, preferred_element_type=F32)
    return f(ah, bh) + (f(ah, bl) + f(al, bh))


def call(kernel, out_shape, us, mib=8, **kw):
    cost = pl.CostEstimate(flops=int(us * 1e9), bytes_accessed=1024, transcendentals=0)
    params = pltpu.CompilerParams(vmem_limit_bytes=mib * 1024 * 1024)
    return pl.pallas_call(kernel, out_shape=out_shape, cost_estimate=cost, compiler_params=params, **kw)


def f32(*shape):
    return jax.ShapeDtypeStruct(shape, F32)


def invert2(a, b, d):
    scale = 1.0 / (a * d - b * b)
    return d * scale, -(b * scale), a * scale


def invert4(d):
    a00, a01, a11 = invert2(d[0][0], d[0][1], d[1][1])
    a = ((a00, a01), (a01, a11))
    t = [[a[i][0] * d[0][j] + a[i][1] * d[1][j] for j in (2, 3)] for i in (0, 1)]
    s = lambda i, j: d[i][j] - (d[0][i] * t[0][j - 2] + d[1][i] * t[1][j - 2])
    s00, s01, s11 = invert2(s(2, 2), s(2, 3), s(3, 3))
    c = ((s00, s01), (s01, s11))
    u = [[t[i][0] * c[0][j] + t[i][1] * c[1][j] for j in (0, 1)] for i in (0, 1)]
    top = [[a[i][j] + (u[i][0] * t[j][0] + u[i][1] * t[j][1]) for j in (0, 1)] for i in (0, 1)]
    top[1][0] = top[0][1]
    return [
        [top[0][0], top[0][1], -u[0][0], -u[0][1]],
        [top[1][0], top[1][1], -u[1][0], -u[1][1]],
        [-u[0][0], -u[1][0], s00, s01],
        [-u[0][1], -u[1][1], s01, s11],
    ]


def sweep_all(block):
    n, group, size = 128, 16, 4
    lane = lax.broadcasted_iota(jnp.int32, (8, n), 1)
    line = lax.broadcasted_iota(jnp.int32, (8, n), 0)
    tiles = n // 8

    def column(tile, k):
        return jnp.broadcast_to(tile[:, k : k + 1], (8, n))

    def step(_, s):
        s = list(s)
        for k in range(0, group, size):
            own, sub = k // 8, k % 8
            rows = [jnp.broadcast_to(s[own][sub + i : sub + i + 1, :], (8, n)) for i in range(size)]
            d = [[column(rows[i], k + j) if j >= i else None for j in range(size)] for i in range(size)]
            inverse = invert4(d)
            scaled = []
            for i in range(size):
                e = inverse[i]
                q = (e[0] * rows[0] + e[1] * rows[1]) + (e[2] * rows[2] + e[3] * rows[3])
                for j in range(size):
                    q = jnp.where(lane == k + j, -e[j], q)
                scaled.append(q)
            pivots = (lane >= k) & (lane < k + size)
            for u in range(tiles):
                c = [column(s[u], k + i) for i in range(size)]
                change = (c[0] * scaled[0] + c[1] * scaled[1]) + (c[2] * scaled[2] + c[3] * scaled[3])
                new = jnp.where(pivots, 0.0, s[u]) - change
                if u == own:
                    for i in range(size):
                        new = jnp.where(line == sub + i, scaled[i], new)
                s[u] = new
        s = s[group // 8 :] + s[: group // 8]
        return tuple(pltpu.roll(v, n - group, 1) for v in s)

    out = lax.fori_loop(0, n // group, step, tuple(block[8 * u : 8 * u + 8, :] for u in range(tiles)))
    return jnp.concatenate(out, axis=0)


def invert_first(gram_ref, ai_ref, t_ref, schur_ref):
    def part(lo, lanes):
        return jnp.concatenate([gram_ref[m, 32 * lanes : 32 * lanes + 32, :] for m in range(lo, lo + 4)], axis=0)

    b = part(0, 1)
    ai = -sweep_all(part(0, 0))
    t = dot(ai, b)
    ai_ref[...] = ai
    t_ref[...] = t
    schur_ref[...] = part(4, 1) - dot(b, t, TN)


def invert_second(ai_ref, t_ref, schur_ref, out_ref):
    h = B // 2
    t = t_ref[...]
    si = -sweep_all(schur_ref[...])
    u = dot(t, si)
    out_ref[:h, :h] = ai_ref[...] + dot(u, t, NT)
    out_ref[:h, h:] = -u
    out_ref[h:, :h] = -u.T
    out_ref[h:, h:] = si


def choose_kernel(col_ref, *refs):
    parts, (out_ref, turned_ref) = refs[:8], refs[8:]
    mine = parts[0][...]
    for k in range(1, 8):
        mine = jnp.where(col_ref[0] == k, parts[k][...], mine)
    for k in range(8):
        out_ref[k] = mine
    turned_ref[...] = mine.T


def gram_kernel(panel_ref, block_ref, out_ref, turned_ref):
    turned = panel_ref[...].T
    gram = dot(turned, panel_ref[...]).reshape(8, 32, B)
    for m in range(8):
        out_ref[m, :256, :] = block_ref[...]
    out_ref[:, 256:288, :] = gram[:, :, :128]
    out_ref[:, 288:, :] = gram[:, :, 128:]
    turned_ref[:256], turned_ref[256:] = split(turned)


def panel_product(turned_ref, right):
    hi, lo = split(right)
    both = lax.dot_general(turned_ref[...], hi, NN, preferred_element_type=F32)
    return both[:256] + (both[256:] + lax.dot_general(turned_ref[:256], lo, NN, preferred_element_type=F32))


def product_kernel(core_ref, turned_ref, theirs_ref, mine_ref, vectors_ref, give_ref, keep_ref):
    step = pl.program_id(0)
    for matrix_ref, out_ref in ((theirs_ref, give_ref), (mine_ref, keep_ref)):
        product = panel_product(turned_ref, matrix_ref[...])
        out_ref[2 * step, :256, :] = product[:, :128]
        out_ref[2 * step + 1, :256, :] = product[:, 128:]
    mixing = panel_product(turned_ref, vectors_ref[...])
    for b in range(2):
        first, last = mixing[:128, 128 * b : 128 * b + 128], mixing[128:, 128 * b : 128 * b + 128]
        first, last = first.reshape(8, 16, 128), last.reshape(8, 16, 128)
        place = pl.multiple_of(32 * step + 16 * b, 16)
        keep_ref[:, pl.ds(256 + place, 16), :] = jnp.where(core_ref[0] == 0, first, last)
        give_ref[:, pl.ds(256 + place, 16), :] = jnp.where(core_ref[0] == 0, last, first)


def join_kernel(keep_ref, got_ref, gram_ref, other_ref, out_ref):
    out_ref[:, :384, :] = keep_ref[...] + got_ref[...]
    gram = gram_ref[...] + other_ref[...]
    for m in range(8):
        out_ref[m, 384:, :] = gram


def reduce_kernel(in_ref, product_ref, own_ref, gram_ref):
    own = in_ref[0, :384, :]
    for m in range(1, 8):
        own = own + in_ref[m, :384, :]
    product_ref[...] = own[:256].T
    own_ref[...] = own
    gram_ref[...] = in_ref[:, 384:, :]


def coupling_kernel(panel_ref, product_ref, out_ref):
    total = jnp.zeros((B, B), F32)
    for m in range(0, 8, 2):
        left = jnp.concatenate([panel_ref[m], panel_ref[m + 1]], axis=1)
        right = jnp.concatenate([product_ref[m], product_ref[m + 1]], axis=1)
        total = total + dot3(split(left), split(right), NT)
    out_ref[...] = total.reshape(16, 16, B)


def sum_kernel(in_ref, out_ref):
    total = jnp.sum(in_ref[...], axis=0)
    for m in range(out_ref.shape[0]):
        out_ref[m] = total


def scale_kernel(panel_ref, product_ref, inverse_ref, left_ref, out_ref):
    inverse = inverse_ref[...]
    hi, lo = split(2.0 * dot(panel_ref[...], inverse))
    left_ref[:, :256], left_ref[:, 256:512], left_ref[:, 512:] = hi, hi, lo
    for k in range(4):
        out_ref[k] = 2.0 * dot(product_ref[k], inverse)


def rotate_kernel(core_ref, left_ref, mine_ref, other_ref, vectors_ref, *out):
    out_ref = out[-1]
    core = core_ref[0]
    mine, other = mine_ref[...], other_ref[...]
    both = jnp.where(core == 0, mine, other), jnp.where(core == 0, other, mine)
    lanes = [jnp.concatenate([h[:, k : k + 16, :].reshape(128, 128) for h in both], axis=0) for k in (0, 16)]
    hi, lo = split(jnp.concatenate(lanes, axis=1))
    right = jnp.concatenate([hi, lo, hi], axis=0)
    out_ref[...] = vectors_ref[...] - lax.dot_general(left_ref[...], right, NN, preferred_element_type=F32)


def update_kernel(
    where_ref, first_ref, near_ref, far_ref, inverse_ref, coupling_ref,
    mine_ref, other_ref, pmine_ref, pother_ref, matrix_ref, out_ref, left_ref, product_ref,
):
    step = pl.program_id(0)

    @pl.when(step == 0)
    def _():
        for k in range(4):
            for piece_ref, zh in ((near_ref, where_ref[2]), (far_ref, 1 - where_ref[2])):
                place = (lax.rem(where_ref[1] + k, 4) * 2 + zh) * 128
                product_ref[pl.ds(pl.multiple_of(place, 128), 128), :] = piece_ref[k]
        small = dot(coupling_ref[...].reshape(B, B), inverse_ref[...])
        hi, lo = split(small)
        right = jnp.concatenate([hi, lo, hi], axis=0)
        u = product_ref[...] - 2.0 * lax.dot_general(first_ref[...], right, NN, preferred_element_type=F32)
        hi, lo = split(u)
        left_ref[:, :768] = first_ref[...]
        left_ref[:, 768:1024], left_ref[:, 1024:1280], left_ref[:, 1280:] = hi, hi, lo

    mine = step // 2 == where_ref[0]
    product = jnp.where(mine, mine_ref[...], other_ref[...])
    panel = jnp.where(mine, pmine_ref[...], pother_ref[...])
    halves = [split(jnp.concatenate([a[m] for m in range(4)], axis=1)) for a in (product, panel)]
    right = jnp.concatenate([x for hi, lo in halves for x in (hi, lo, hi)], axis=0)
    out_ref[...] = matrix_ref[...] - lax.dot_general(left_ref[...], right, NN, preferred_element_type=F32)


def repeat(block, n=8):
    return jnp.broadcast_to(block[None], (n,) + block.shape)


def exchange(blocks, axes):
    return lax.all_to_all(blocks, axes, 0, 0, tiled=True)


def swap_cores(array):
    return lax.ppermute(array, "co", [(0, 1), (1, 0)])


def gather_x(block):
    return jnp.stack([block] + [lax.ppermute(block, "x", [((x + k) % 4, x) for x in range(4)]) for k in (1, 2, 3)])


def flip_pairs():
    pairs = []
    for i in range(16):
        for k in range(8):
            pairs.append((i * 8 + k, (k * 2 + i % 2) * 8 + i // 2))
    return pairs


VMEM = pl.BlockSpec(memory_space=pltpu.VMEM)
SMEM = pl.BlockSpec(memory_space=pltpu.SMEM)


def whole(*shape):
    return pl.BlockSpec(shape, lambda t: (0,) * len(shape))


def fixed(*shape):
    return pl.BlockSpec(shape, lambda t, w: (0,) * len(shape))


def rotate(at, core, first, final, other, vectors, *done):
    mixing = pl.BlockSpec((8, 32, 128), lambda t: (0, 8 + at + t, 0))
    tile = pl.BlockSpec((1024, 256), lambda t: (0, at + t))
    return call(
        rotate_kernel,
        f32(1024, 1024),
        3,
        60,
        grid=(2,),
        in_specs=[SMEM, whole(1024, 768), mixing, mixing, tile] + [pl.BlockSpec(memory_space=pl.ANY)] * len(done),
        out_specs=tile,
        input_output_aliases={5: 0} if done else {},
    )(core, first, final, other, vectors, *done)


def body(matrix, vectors):
    rows_here = matrix.shape[0]
    row_index = lax.axis_index(ROW)
    col_index = lax.axis_index(COL)
    core = lax.axis_index("co").astype(jnp.int32).reshape(1)
    where = jnp.stack([core[0], lax.axis_index("x").astype(jnp.int32), lax.axis_index("zh").astype(jnp.int32)])
    there = flip_pairs()
    back = [(b, a) for a, b in there]

    global_rows = row_index * rows_here + jnp.arange(rows_here, dtype=jnp.int32)
    columns = jnp.where(global_rows[:, None] >= B, matrix[:, :B], F32(0.0))
    parts = [columns[:128]]
    for k in range(1, 8):
        parts.append(lax.ppermute(columns[k * 128 : (k + 1) * 128], COL, [(0, k)]))
    sent, turned = call(
        choose_kernel, (f32(8, 128, 256), f32(256, 128)), 1, in_specs=[SMEM] + [VMEM] * 8
    )(col_index.astype(jnp.int32).reshape(1), *parts)
    turned = lax.ppermute(turned, ALL, there)
    panel_rows = exchange(sent, COL).reshape(1024, B)
    sent, stacked = call(gram_kernel, (f32(8, 320, 128), jax.ShapeDtypeStruct((512, 1024), BF16)), 2, 12)(
        panel_rows, turned
    )
    panel = exchange(sent, CHIPS)
    half = pl.BlockSpec((8, 384, 128), lambda t, core: (0, 0, 0))
    give, keep = call(
        product_kernel,
        (f32(8, 384, 128), f32(8, 384, 128)),
        12,
        60,
        grid_spec=pltpu.PrefetchScalarGridSpec(
            num_scalar_prefetch=1,
            grid=(4,),
            in_specs=[
                pl.BlockSpec((512, 1024), lambda t, core: (0, 0)),
                pl.BlockSpec((1024, 256), lambda t, core: (0, (1 - core[0]) * 4 + t)),
                pl.BlockSpec((1024, 256), lambda t, core: (0, core[0] * 4 + t)),
                pl.BlockSpec((1024, 256), lambda t, core: (0, t)),
            ],
            out_specs=(half, half),
        ),
    )(core, stacked, matrix, matrix, vectors)
    give, keep, panel = lax.optimization_barrier((give, keep, panel))
    got = swap_cores(give)
    gram = jnp.sum(panel[:, 256:], axis=0)
    other_gram = swap_cores(gram)
    other_panel = swap_cores(panel)
    came = exchange(call(join_kernel, f32(8, 448, 128), 1, 12)(keep, got, gram, other_gram), CHIPS)

    product, own, gram = call(reduce_kernel, (f32(128, 256), f32(384, 128), f32(8, 64, 128)), 2, 12)(came)
    final = exchange(repeat(own), CHIPS)
    near = gather_x(lax.ppermute(product, ALL, back))
    ai, t, schur = call(invert_first, (f32(128, 128),) * 3, 9)(gram)
    inverse = call(invert_second, f32(B, B), 9)(ai, t, schur)
    first, near = call(
        scale_kernel, (jax.ShapeDtypeStruct((1024, 768), BF16), f32(4, 128, 256)), 4, 20
    )(panel_rows, near, inverse)
    final, near, first, inverse = lax.optimization_barrier((final, near, first, inverse))
    other = swap_cores(final)
    far = lax.ppermute(near, "zh", [(0, 1), (1, 0)])
    coupling = call(
        coupling_kernel,
        f32(16, 16, 256),
        2,
        grid=(1,),
        in_specs=[
            pl.BlockSpec((8, 256, 128), lambda t: (0, 0, 0)),
            pl.BlockSpec((8, 256, 128), lambda t: (0, 0, 0)),
        ],
        out_specs=whole(16, 16, 256),
    )(panel, final)
    rotated = rotate(0, core, first, final, other, vectors)
    coupling, rotated = lax.optimization_barrier((exchange(coupling, COUPLED), rotated))
    coupling = exchange(call(sum_kernel, f32(16, 16, 256), 1)(coupling), COUPLED)
    rotated = rotate(2, core, first, final, other, vectors, rotated)
    coupling, rotated = lax.optimization_barrier((coupling, rotated))

    mine = pl.BlockSpec((4, 256, 128), lambda t, w: (jnp.clip(t - 2 * w[0], 0, 1), 0, 0))
    theirs = pl.BlockSpec((4, 256, 128), lambda t, w: (jnp.clip(t - 2 * (1 - w[0]), 0, 1), 0, 0))
    piece = fixed(4, 128, 256)
    updated = call(
        update_kernel,
        f32(1024, 2048),
        12,
        60,
        grid_spec=pltpu.PrefetchScalarGridSpec(
            num_scalar_prefetch=1,
            grid=(4,),
            in_specs=[
                fixed(1024, 768), piece, piece, fixed(256, 256), fixed(16, 16, 256), mine, theirs, mine, theirs,
                pl.BlockSpec((1024, 512), lambda t, w: (0, t)),
            ],
            out_specs=pl.BlockSpec((1024, 512), lambda t, w: (0, t)),
            scratch_shapes=[pltpu.VMEM((1024, 1536), BF16), pltpu.VMEM((1024, 256), F32)],
        ),
    )(where, first, near, far, inverse, coupling, final, other, panel, other_panel, matrix)
    return (updated, rotated)


def solution(mesh):
    fine = Mesh(mesh.devices.reshape(4, 2, 2, 4, 2), ALL)
    placed = (P(ROW, COL), P(ROW, COL))
    return jax.shard_map(body, mesh=fine, in_specs=placed, out_specs=placed, check_vma=False)
```

```python
import jax
import jax.numpy as jnp
from jax import lax
from jax.experimental import pallas as pl
from jax.experimental.pallas import tpu as pltpu
from jax.sharding import Mesh
from jax.sharding import PartitionSpec as P

B = 256
ROW = ("y", "zl", "co")
CHIPS = ("y", "zl")
COL = ("x", "zh")
COUPLED = ("co", "x", "zh")
ALL = ("y", "zl", "co", "x", "zh")
HIGHEST = lax.Precision.HIGHEST
F32 = jnp.float32
ORDER = (0, 1, 6, 2, 5, 7, 3, 4)
BF16 = jnp.bfloat16
NN = (((1,), (0,)), ((), ()))
NT = (((1,), (1,)), ((), ()))
TN = (((0,), (0,)), ((), ()))


def dot(left, right, dims=NN):
    return lax.dot_general(left, right, dims, preferred_element_type=F32, precision=HIGHEST)


def split(x):
    hi = x.astype(BF16)
    return hi, (x - hi.astype(F32)).astype(BF16)


def dot3(left, right, dims=NN):
    (ah, al), (bh, bl) = left, right
    f = lambda a, b: lax.dot_general(a, b, dims, preferred_element_type=F32)
    return f(ah, bh) + (f(ah, bl) + f(al, bh))


def call(kernel, out_shape, us, mib=8, **kw):
    cost = pl.CostEstimate(flops=int(us * 1e9), bytes_accessed=1024, transcendentals=0)
    params = pltpu.CompilerParams(vmem_limit_bytes=mib * 1024 * 1024)
    return pl.pallas_call(kernel, out_shape=out_shape, cost_estimate=cost, compiler_params=params, **kw)


def f32(*shape):
    return jax.ShapeDtypeStruct(shape, F32)


def invert2(a, b, d):
    scale = 1.0 / (a * d - b * b)
    return d * scale, -(b * scale), a * scale


def invert4(d):
    a00, a01, a11 = invert2(d[0][0], d[0][1], d[1][1])
    a = ((a00, a01), (a01, a11))
    t = [[a[i][0] * d[0][j] + a[i][1] * d[1][j] for j in (2, 3)] for i in (0, 1)]
    s = lambda i, j: d[i][j] - (d[0][i] * t[0][j - 2] + d[1][i] * t[1][j - 2])
    s00, s01, s11 = invert2(s(2, 2), s(2, 3), s(3, 3))
    c = ((s00, s01), (s01, s11))
    u = [[t[i][0] * c[0][j] + t[i][1] * c[1][j] for j in (0, 1)] for i in (0, 1)]
    top = [[a[i][j] + (u[i][0] * t[j][0] + u[i][1] * t[j][1]) for j in (0, 1)] for i in (0, 1)]
    top[1][0] = top[0][1]
    return [
        [top[0][0], top[0][1], -u[0][0], -u[0][1]],
        [top[1][0], top[1][1], -u[1][0], -u[1][1]],
        [-u[0][0], -u[1][0], s00, s01],
        [-u[0][1], -u[1][1], s01, s11],
    ]


def sweep_all(block):
    n, group, size = 128, 16, 4
    lane = lax.broadcasted_iota(jnp.int32, (8, n), 1)
    line = lax.broadcasted_iota(jnp.int32, (8, n), 0)
    tiles = n // 8

    def column(tile, k):
        return jnp.broadcast_to(tile[:, k : k + 1], (8, n))

    def step(_, s):
        s = list(s)
        for k in range(0, group, size):
            own, sub = k // 8, k % 8
            rows = [jnp.broadcast_to(s[own][sub + i : sub + i + 1, :], (8, n)) for i in range(size)]
            d = [[column(rows[i], k + j) if j >= i else None for j in range(size)] for i in range(size)]
            inverse = invert4(d)
            scaled = []
            for i in range(size):
                e = inverse[i]
                q = (e[0] * rows[0] + e[1] * rows[1]) + (e[2] * rows[2] + e[3] * rows[3])
                for j in range(size):
                    q = jnp.where(lane == k + j, -e[j], q)
                scaled.append(q)
            pivots = (lane >= k) & (lane < k + size)
            for u in range(tiles):
                c = [column(s[u], k + i) for i in range(size)]
                change = (c[0] * scaled[0] + c[1] * scaled[1]) + (c[2] * scaled[2] + c[3] * scaled[3])
                new = jnp.where(pivots, 0.0, s[u]) - change
                if u == own:
                    for i in range(size):
                        new = jnp.where(line == sub + i, scaled[i], new)
                s[u] = new
        s = s[group // 8 :] + s[: group // 8]
        return tuple(pltpu.roll(v, n - group, 1) for v in s)

    out = lax.fori_loop(0, n // group, step, tuple(block[8 * u : 8 * u + 8, :] for u in range(tiles)))
    return jnp.concatenate(out, axis=0)


def invert_first(gram_ref, ai_ref, t_ref, schur_ref):
    def part(lo, lanes):
        return jnp.concatenate([gram_ref[m, 32 * lanes : 32 * lanes + 32, :] for m in range(lo, lo + 4)], axis=0)

    b = part(0, 1)
    ai = -sweep_all(part(0, 0))
    t = dot(ai, b)
    ai_ref[...] = ai
    t_ref[...] = t
    schur_ref[...] = part(4, 1) - dot(b, t, TN)


def invert_second(ai_ref, t_ref, schur_ref, out_ref):
    h = B // 2
    t = t_ref[...]
    si = -sweep_all(schur_ref[...])
    u = dot(t, si)
    out_ref[:h, :h] = ai_ref[...] + dot(u, t, NT)
    out_ref[:h, h:] = -u
    out_ref[h:, :h] = -u.T
    out_ref[h:, h:] = si


def choose_kernel(col_ref, *refs):
    parts, (out_ref, turned_ref) = refs[:8], refs[8:]
    mine = parts[0][...]
    for k, part in zip(ORDER[1:], parts[1:]):
        mine = jnp.where(col_ref[0] == k, part[...], mine)
    for k in range(8):
        out_ref[k] = mine
    turned_ref[...] = mine.T


def gram_kernel(panel_ref, block_ref, out_ref):
    gram = dot(panel_ref[...].T, panel_ref[...]).reshape(8, 32, B)
    for m in range(8):
        out_ref[m, :256, :] = block_ref[...]
    out_ref[:, 256:288, :] = gram[:, :, :128]
    out_ref[:, 288:, :] = gram[:, :, 128:]


def panel_product(turned_ref, right):
    hi, lo = split(right)
    both = lax.dot_general(turned_ref[...], hi, NN, preferred_element_type=F32)
    return both[:256] + (both[256:] + lax.dot_general(turned_ref[:256], lo, NN, preferred_element_type=F32))


def product_kernel(core_ref, panel_ref, theirs_ref, mine_ref, vectors_ref, give_ref, keep_ref, turned_ref):
    step = pl.program_id(0)

    @pl.when(step == 0)
    def _():
        turned_ref[:256], turned_ref[256:] = split(panel_ref[...].T)

    for matrix_ref, out_ref in ((theirs_ref, give_ref), (mine_ref, keep_ref)):
        product = panel_product(turned_ref, matrix_ref[...])
        out_ref[2 * step, :256, :] = product[:, :128]
        out_ref[2 * step + 1, :256, :] = product[:, 128:]
    mixing = panel_product(turned_ref, vectors_ref[...])
    for b in range(2):
        first, last = mixing[:128, 128 * b : 128 * b + 128], mixing[128:, 128 * b : 128 * b + 128]
        first, last = first.reshape(8, 16, 128), last.reshape(8, 16, 128)
        place = pl.multiple_of(32 * step + 16 * b, 16)
        keep_ref[:, pl.ds(256 + place, 16), :] = jnp.where(core_ref[0] == 0, first, last)
        give_ref[:, pl.ds(256 + place, 16), :] = jnp.where(core_ref[0] == 0, last, first)


def join_kernel(keep_ref, got_ref, gram_ref, other_ref, out_ref):
    out_ref[:, :384, :] = keep_ref[...] + got_ref[...]
    gram = gram_ref[...] + other_ref[...]
    for m in range(8):
        out_ref[m, 384:, :] = gram


def reduce_kernel(in_ref, product_ref, own_ref, gram_ref):
    own = in_ref[0, :384, :]
    for m in range(1, 8):
        own = own + in_ref[m, :384, :]
    product_ref[...] = own[:256].T
    own_ref[...] = own
    gram_ref[...] = in_ref[:, 384:, :]


def coupling_kernel(panel_ref, product_ref, out_ref):
    total = jnp.zeros((B, B), F32)
    for m in range(0, 8, 2):
        left = jnp.concatenate([panel_ref[m], panel_ref[m + 1]], axis=1)
        right = jnp.concatenate([product_ref[m], product_ref[m + 1]], axis=1)
        total = total + dot3(split(left), split(right), NT)
    out_ref[...] = total.reshape(16, 16, B)


def sum_kernel(in_ref, out_ref):
    total = jnp.sum(in_ref[...], axis=0)
    for m in range(out_ref.shape[0]):
        out_ref[m] = total


def scale_kernel(panel_ref, product_ref, inverse_ref, left_ref, out_ref):
    inverse = inverse_ref[...]
    hi, lo = split(2.0 * dot(panel_ref[...], inverse))
    left_ref[:, :256], left_ref[:, 256:512], left_ref[:, 512:] = hi, hi, lo
    for k in range(4):
        out_ref[k] = 2.0 * dot(product_ref[k], inverse)


def rotate_kernel(core_ref, left_ref, mine_ref, other_ref, vectors_ref, *out):
    out_ref = out[-1]
    core = core_ref[0]
    mine, other = mine_ref[...], other_ref[...]
    both = jnp.where(core == 0, mine, other), jnp.where(core == 0, other, mine)
    lanes = [jnp.concatenate([h[:, k : k + 16, :].reshape(128, 128) for h in both], axis=0) for k in (0, 16)]
    hi, lo = split(jnp.concatenate(lanes, axis=1))
    right = jnp.concatenate([hi, lo, hi], axis=0)
    out_ref[...] = vectors_ref[...] - lax.dot_general(left_ref[...], right, NN, preferred_element_type=F32)


def update_kernel(
    where_ref, first_ref, near_ref, far_ref, inverse_ref, coupling_ref,
    mine_ref, other_ref, pmine_ref, pother_ref, matrix_ref, out_ref, left_ref, product_ref,
):
    step = pl.program_id(0)

    @pl.when(step == 0)
    def _():
        for k in range(4):
            for piece_ref, zh in ((near_ref, where_ref[2]), (far_ref, 1 - where_ref[2])):
                place = (lax.rem(where_ref[1] + k, 4) * 2 + zh) * 128
                product_ref[pl.ds(pl.multiple_of(place, 128), 128), :] = piece_ref[k]
        small = dot(coupling_ref[...].reshape(B, B), inverse_ref[...])
        hi, lo = split(small)
        right = jnp.concatenate([hi, lo, hi], axis=0)
        u = product_ref[...] - 2.0 * lax.dot_general(first_ref[...], right, NN, preferred_element_type=F32)
        hi, lo = split(u)
        left_ref[:, :768] = first_ref[...]
        left_ref[:, 768:1024], left_ref[:, 1024:1280], left_ref[:, 1280:] = hi, hi, lo

    mine = step // 2 == where_ref[0]
    product = jnp.where(mine, mine_ref[...], other_ref[...])
    panel = jnp.where(mine, pmine_ref[...], pother_ref[...])
    halves = [split(jnp.concatenate([a[m] for m in range(4)], axis=1)) for a in (product, panel)]
    right = jnp.concatenate([x for hi, lo in halves for x in (hi, lo, hi)], axis=0)
    out_ref[...] = matrix_ref[...] - lax.dot_general(left_ref[...], right, NN, preferred_element_type=F32)


def repeat(block, n=8):
    return jnp.broadcast_to(block[None], (n,) + block.shape)


def exchange(blocks, axes):
    return lax.all_to_all(blocks, axes, 0, 0, tiled=True)


def swap_cores(array):
    return lax.ppermute(array, "co", [(0, 1), (1, 0)])


def gather_x(block):
    return jnp.stack([block] + [lax.ppermute(block, "x", [((x + k) % 4, x) for x in range(4)]) for k in (1, 2, 3)])


def flip_pairs():
    pairs = []
    for i in range(16):
        for k in range(8):
            pairs.append((i * 8 + k, (k * 2 + i % 2) * 8 + i // 2))
    return pairs


VMEM = pl.BlockSpec(memory_space=pltpu.VMEM)
SMEM = pl.BlockSpec(memory_space=pltpu.SMEM)


def whole(*shape):
    return pl.BlockSpec(shape, lambda t: (0,) * len(shape))


def fixed(*shape):
    return pl.BlockSpec(shape, lambda t, w: (0,) * len(shape))


def rotate(at, core, first, final, other, vectors, *done):
    mixing = pl.BlockSpec((8, 32, 128), lambda t: (0, 8 + at + t, 0))
    tile = pl.BlockSpec((1024, 256), lambda t: (0, at + t))
    return call(
        rotate_kernel,
        f32(1024, 1024),
        3,
        60,
        grid=(2,),
        in_specs=[SMEM, whole(1024, 768), mixing, mixing, tile] + [pl.BlockSpec(memory_space=pl.ANY)] * len(done),
        out_specs=tile,
        input_output_aliases={5: 0} if done else {},
    )(core, first, final, other, vectors, *done)


def body(matrix, vectors):
    rows_here = matrix.shape[0]
    row_index = lax.axis_index(ROW)
    col_index = lax.axis_index(COL)
    core = lax.axis_index("co").astype(jnp.int32).reshape(1)
    where = jnp.stack([core[0], lax.axis_index("x").astype(jnp.int32), lax.axis_index("zh").astype(jnp.int32)])
    there = flip_pairs()
    back = [(b, a) for a, b in there]

    global_rows = row_index * rows_here + jnp.arange(rows_here, dtype=jnp.int32)
    columns = jnp.where(global_rows[:, None] >= B, matrix[:, :B], F32(0.0))
    parts = {0: columns[:128]}
    for k in ORDER[1:]:
        parts[k] = lax.ppermute(columns[k * 128 : (k + 1) * 128], COL, [(0, k)])
    sent, turned = call(
        choose_kernel, (f32(8, 128, 256), f32(256, 128)), 1, in_specs=[SMEM] + [VMEM] * 8
    )(col_index.astype(jnp.int32).reshape(1), *(parts[k] for k in ORDER))
    turned = lax.ppermute(turned, ALL, there)
    panel_rows = exchange(sent, COL).reshape(1024, B)
    sent = call(gram_kernel, f32(8, 320, 128), 2, 12)(panel_rows, turned)
    panel = exchange(sent, CHIPS)
    half = pl.BlockSpec((8, 384, 128), lambda t, core: (0, 0, 0))
    give, keep = call(
        product_kernel,
        (f32(8, 384, 128), f32(8, 384, 128)),
        12,
        60,
        grid_spec=pltpu.PrefetchScalarGridSpec(
            num_scalar_prefetch=1,
            grid=(4,),
            in_specs=[
                pl.BlockSpec((1024, 256), lambda t, core: (0, 0)),
                pl.BlockSpec((1024, 256), lambda t, core: (0, (1 - core[0]) * 4 + t)),
                pl.BlockSpec((1024, 256), lambda t, core: (0, core[0] * 4 + t)),
                pl.BlockSpec((1024, 256), lambda t, core: (0, t)),
            ],
            out_specs=(half, half),
            scratch_shapes=[pltpu.VMEM((512, 1024), BF16)],
        ),
    )(core, panel_rows, matrix, matrix, vectors)
    give, keep, panel, where = lax.optimization_barrier((give, keep, panel, where))
    got = swap_cores(give)
    gram = jnp.sum(panel[:, 256:], axis=0)
    other_gram = swap_cores(gram)
    other_panel = swap_cores(panel)
    came = exchange(call(join_kernel, f32(8, 448, 128), 1, 12)(keep, got, gram, other_gram), CHIPS)

    product, own, gram = call(reduce_kernel, (f32(128, 256), f32(384, 128), f32(8, 64, 128)), 2, 12)(came)
    final = exchange(repeat(own), CHIPS)
    near = gather_x(lax.ppermute(product, ALL, back))
    ai, t, schur = call(invert_first, (f32(128, 128),) * 3, 9)(gram)
    inverse = call(invert_second, f32(B, B), 9)(ai, t, schur)
    first, near = call(
        scale_kernel, (jax.ShapeDtypeStruct((1024, 768), BF16), f32(4, 128, 256)), 4, 20
    )(panel_rows, near, inverse)
    final, near, first, inverse = lax.optimization_barrier((final, near, first, inverse))
    other = swap_cores(final)
    far = lax.ppermute(near, "zh", [(0, 1), (1, 0)])
    coupling = call(
        coupling_kernel,
        f32(16, 16, 256),
        2,
        grid=(1,),
        in_specs=[
            pl.BlockSpec((8, 256, 128), lambda t: (0, 0, 0)),
            pl.BlockSpec((8, 256, 128), lambda t: (0, 0, 0)),
        ],
        out_specs=whole(16, 16, 256),
    )(panel, final)
    rotated = rotate(0, core, first, final, other, vectors)
    coupling, rotated = lax.optimization_barrier((exchange(coupling, COUPLED), rotated))
    coupling = exchange(call(sum_kernel, f32(16, 16, 256), 1)(coupling), COUPLED)
    rotated = rotate(2, core, first, final, other, vectors, rotated)
    coupling, rotated = lax.optimization_barrier((coupling, rotated))

    mine = pl.BlockSpec((4, 256, 128), lambda t, w: (jnp.clip(t - 2 * w[0], 0, 1), 0, 0))
    theirs = pl.BlockSpec((4, 256, 128), lambda t, w: (jnp.clip(t - 2 * (1 - w[0]), 0, 1), 0, 0))
    piece = fixed(4, 128, 256)
    updated = call(
        update_kernel,
        f32(1024, 2048),
        12,
        60,
        grid_spec=pltpu.PrefetchScalarGridSpec(
            num_scalar_prefetch=1,
            grid=(4,),
            in_specs=[
                fixed(1024, 768), piece, piece, fixed(256, 256), fixed(16, 16, 256), mine, theirs, mine, theirs,
                pl.BlockSpec((1024, 512), lambda t, w: (0, t)),
            ],
            out_specs=pl.BlockSpec((1024, 512), lambda t, w: (0, t)),
            scratch_shapes=[pltpu.VMEM((1024, 1536), BF16), pltpu.VMEM((1024, 256), F32)],
        ),
    )(where, first, near, far, inverse, coupling, final, other, panel, other_panel, matrix)
    return (updated, rotated)


def solution(mesh):
    fine = Mesh(mesh.devices.reshape(4, 2, 2, 4, 2), ALL)
    placed = (P(ROW, COL), P(ROW, COL))
    return jax.shard_map(body, mesh=fine, in_specs=placed, out_specs=placed, check_vma=False)
```

```python
import jax
import jax.numpy as jnp
from jax import lax
from jax.experimental import pallas as pl
from jax.experimental.pallas import tpu as pltpu
from jax.sharding import Mesh
from jax.sharding import PartitionSpec as P

B = 256
ROW = ("y", "zl", "co")
CHIPS = ("y", "zl")
COL = ("x", "zh")
COUPLED = ("co", "x", "zh")
ALL = ("y", "zl", "co", "x", "zh")
HIGHEST = lax.Precision.HIGHEST
F32 = jnp.float32
ORDER = (0, 1, 6, 2, 5, 7, 3, 4)
BF16 = jnp.bfloat16
NN = (((1,), (0,)), ((), ()))
NT = (((1,), (1,)), ((), ()))
TN = (((0,), (0,)), ((), ()))


def dot(left, right, dims=NN):
    return lax.dot_general(left, right, dims, preferred_element_type=F32, precision=HIGHEST)


def split(x):
    hi = x.astype(BF16)
    return hi, (x - hi.astype(F32)).astype(BF16)


def dot3(left, right, dims=NN):
    (ah, al), (bh, bl) = left, right
    f = lambda a, b: lax.dot_general(a, b, dims, preferred_element_type=F32)
    return f(ah, bh) + (f(ah, bl) + f(al, bh))


def call(kernel, out_shape, us, mib=8, **kw):
    cost = pl.CostEstimate(flops=int(us * 1e9), bytes_accessed=1024, transcendentals=0)
    params = pltpu.CompilerParams(vmem_limit_bytes=mib * 1024 * 1024)
    return pl.pallas_call(kernel, out_shape=out_shape, cost_estimate=cost, compiler_params=params, **kw)


def f32(*shape):
    return jax.ShapeDtypeStruct(shape, F32)


def invert2(a, b, d):
    scale = 1.0 / (a * d - b * b)
    return d * scale, -(b * scale), a * scale


def invert4(d):
    a00, a01, a11 = invert2(d[0][0], d[0][1], d[1][1])
    a = ((a00, a01), (a01, a11))
    t = [[a[i][0] * d[0][j] + a[i][1] * d[1][j] for j in (2, 3)] for i in (0, 1)]
    s = lambda i, j: d[i][j] - (d[0][i] * t[0][j - 2] + d[1][i] * t[1][j - 2])
    s00, s01, s11 = invert2(s(2, 2), s(2, 3), s(3, 3))
    c = ((s00, s01), (s01, s11))
    u = [[t[i][0] * c[0][j] + t[i][1] * c[1][j] for j in (0, 1)] for i in (0, 1)]
    top = [[a[i][j] + (u[i][0] * t[j][0] + u[i][1] * t[j][1]) for j in (0, 1)] for i in (0, 1)]
    top[1][0] = top[0][1]
    return [
        [top[0][0], top[0][1], -u[0][0], -u[0][1]],
        [top[1][0], top[1][1], -u[1][0], -u[1][1]],
        [-u[0][0], -u[1][0], s00, s01],
        [-u[0][1], -u[1][1], s01, s11],
    ]


def sweep_all(block):
    n, group, size = 128, 16, 4
    lane = lax.broadcasted_iota(jnp.int32, (8, n), 1)
    line = lax.broadcasted_iota(jnp.int32, (8, n), 0)
    tiles = n // 8

    def column(tile, k):
        return jnp.broadcast_to(tile[:, k : k + 1], (8, n))

    def step(_, s):
        s = list(s)
        for k in range(0, group, size):
            own, sub = k // 8, k % 8
            rows = [jnp.broadcast_to(s[own][sub + i : sub + i + 1, :], (8, n)) for i in range(size)]
            d = [[column(rows[i], k + j) if j >= i else None for j in range(size)] for i in range(size)]
            inverse = invert4(d)
            scaled = []
            for i in range(size):
                e = inverse[i]
                q = (e[0] * rows[0] + e[1] * rows[1]) + (e[2] * rows[2] + e[3] * rows[3])
                for j in range(size):
                    q = jnp.where(lane == k + j, -e[j], q)
                scaled.append(q)
            pivots = (lane >= k) & (lane < k + size)
            for u in range(tiles):
                c = [column(s[u], k + i) for i in range(size)]
                change = (c[0] * scaled[0] + c[1] * scaled[1]) + (c[2] * scaled[2] + c[3] * scaled[3])
                new = jnp.where(pivots, 0.0, s[u]) - change
                if u == own:
                    for i in range(size):
                        new = jnp.where(line == sub + i, scaled[i], new)
                s[u] = new
        s = s[group // 8 :] + s[: group // 8]
        return tuple(pltpu.roll(v, n - group, 1) for v in s)

    out = lax.fori_loop(0, n // group, step, tuple(block[8 * u : 8 * u + 8, :] for u in range(tiles)))
    return jnp.concatenate(out, axis=0)


def invert_first(gram_ref, ai_ref, t_ref, schur_ref):
    def part(lo, lanes):
        return jnp.concatenate([gram_ref[m, 32 * lanes : 32 * lanes + 32, :] for m in range(lo, lo + 4)], axis=0)

    b = part(0, 1)
    ai = -sweep_all(part(0, 0))
    t = dot(ai, b)
    ai_ref[...] = ai
    t_ref[...] = t
    schur_ref[...] = part(4, 1) - dot(b, t, TN)


def invert_second(ai_ref, t_ref, schur_ref, out_ref):
    h = B // 2
    t = t_ref[...]
    si = -sweep_all(schur_ref[...])
    u = dot(t, si)
    out_ref[:h, :h] = ai_ref[...] + dot(u, t, NT)
    out_ref[:h, h:] = -u
    out_ref[h:, :h] = -u.T
    out_ref[h:, h:] = si


def choose_kernel(col_ref, *refs):
    parts, (out_ref, turned_ref) = refs[:8], refs[8:]
    mine = parts[0][...]
    for k, part in zip(ORDER[1:], parts[1:]):
        mine = jnp.where(col_ref[0] == k, part[...], mine)
    for k in range(8):
        out_ref[k] = mine
    turned_ref[...] = mine.T


def gram_kernel(panel_ref, block_ref, out_ref):
    gram = dot(panel_ref[...].T, panel_ref[...]).reshape(8, 32, B)
    for m in range(8):
        out_ref[m, :256, :] = block_ref[...]
    out_ref[:, 256:288, :] = gram[:, :, :128]
    out_ref[:, 288:, :] = gram[:, :, 128:]


def panel_product(turned_ref, right):
    hi, lo = split(right)
    both = lax.dot_general(turned_ref[...], hi, NN, preferred_element_type=F32)
    return both[:256] + (both[256:] + lax.dot_general(turned_ref[:256], lo, NN, preferred_element_type=F32))


def product_kernel(core_ref, panel_ref, theirs_ref, mine_ref, vectors_ref, give_ref, keep_ref, turned_ref):
    step = pl.program_id(0)

    @pl.when(step == 0)
    def _():
        turned_ref[:256], turned_ref[256:] = split(panel_ref[...].T)

    for matrix_ref, out_ref in ((theirs_ref, give_ref), (mine_ref, keep_ref)):
        product = panel_product(turned_ref, matrix_ref[...])
        out_ref[2 * step, :256, :] = product[:, :128]
        out_ref[2 * step + 1, :256, :] = product[:, 128:]
    mixing = panel_product(turned_ref, vectors_ref[...])
    for b in range(2):
        first, last = mixing[:128, 128 * b : 128 * b + 128], mixing[128:, 128 * b : 128 * b + 128]
        first, last = first.reshape(8, 16, 128), last.reshape(8, 16, 128)
        place = pl.multiple_of(32 * step + 16 * b, 16)
        keep_ref[:, pl.ds(256 + place, 16), :] = jnp.where(core_ref[0] == 0, first, last)
        give_ref[:, pl.ds(256 + place, 16), :] = jnp.where(core_ref[0] == 0, last, first)


def join_kernel(keep_ref, got_ref, gram_ref, other_ref, out_ref):
    out_ref[:, :384, :] = keep_ref[...] + got_ref[...]
    gram = gram_ref[...] + other_ref[...]
    for m in range(8):
        out_ref[m, 384:, :] = gram


def reduce_kernel(in_ref, product_ref, out_ref, gram_ref):
    own = in_ref[0, :384, :]
    for m in range(1, 8):
        own = own + in_ref[m, :384, :]
    product_ref[...] = own[:256].T
    for m in range(8):
        out_ref[m] = own
    gram_ref[...] = in_ref[:, 384:, :]


def coupling_kernel(panel_ref, product_ref, out_ref):
    total = jnp.zeros((B, B), F32)
    for m in range(0, 8, 2):
        left = jnp.concatenate([panel_ref[m], panel_ref[m + 1]], axis=1)
        right = jnp.concatenate([product_ref[m], product_ref[m + 1]], axis=1)
        total = total + dot3(split(left), split(right), NT)
    out_ref[...] = total.reshape(16, 16, B)


def sum_kernel(in_ref, out_ref):
    total = jnp.sum(in_ref[...], axis=0)
    for m in range(out_ref.shape[0]):
        out_ref[m] = total


def scale_kernel(panel_ref, product_ref, inverse_ref, left_ref, out_ref):
    inverse = inverse_ref[...]
    hi, lo = split(2.0 * dot(panel_ref[...], inverse))
    left_ref[:, :256], left_ref[:, 256:512], left_ref[:, 512:] = hi, hi, lo
    for k in range(4):
        out_ref[k] = 2.0 * dot(product_ref[k], inverse)


def rotate_kernel(core_ref, left_ref, mine_ref, other_ref, vectors_ref, *out):
    out_ref = out[-1]
    core = core_ref[0]
    mine, other = mine_ref[...], other_ref[...]
    both = jnp.where(core == 0, mine, other), jnp.where(core == 0, other, mine)
    lanes = [jnp.concatenate([h[:, k : k + 16, :].reshape(128, 128) for h in both], axis=0) for k in (0, 16)]
    hi, lo = split(jnp.concatenate(lanes, axis=1))
    right = jnp.concatenate([hi, lo, hi], axis=0)
    out_ref[...] = vectors_ref[...] - lax.dot_general(left_ref[...], right, NN, preferred_element_type=F32)


def update_kernel(
    where_ref, first_ref, near_ref, far_ref, inverse_ref, coupling_ref,
    mine_ref, other_ref, pmine_ref, pother_ref, matrix_ref, out_ref, left_ref, product_ref,
):
    step = pl.program_id(0)

    @pl.when(step == 0)
    def _():
        for k in range(4):
            for piece_ref, zh in ((near_ref, where_ref[2]), (far_ref, 1 - where_ref[2])):
                place = (lax.rem(where_ref[1] + k, 4) * 2 + zh) * 128
                product_ref[pl.ds(pl.multiple_of(place, 128), 128), :] = piece_ref[k]
        small = dot(coupling_ref[...].reshape(B, B), inverse_ref[...])
        hi, lo = split(small)
        right = jnp.concatenate([hi, lo, hi], axis=0)
        u = product_ref[...] - 2.0 * lax.dot_general(first_ref[...], right, NN, preferred_element_type=F32)
        hi, lo = split(u)
        left_ref[:, :768] = first_ref[...]
        left_ref[:, 768:1024], left_ref[:, 1024:1280], left_ref[:, 1280:] = hi, hi, lo

    mine = step // 2 == where_ref[0]
    product = jnp.where(mine, mine_ref[...], other_ref[...])
    panel = jnp.where(mine, pmine_ref[...], pother_ref[...])
    halves = [split(jnp.concatenate([a[m] for m in range(4)], axis=1)) for a in (product, panel)]
    right = jnp.concatenate([x for hi, lo in halves for x in (hi, lo, hi)], axis=0)
    out_ref[...] = matrix_ref[...] - lax.dot_general(left_ref[...], right, NN, preferred_element_type=F32)


def repeat(block, n=8):
    return jnp.broadcast_to(block[None], (n,) + block.shape)


def exchange(blocks, axes):
    return lax.all_to_all(blocks, axes, 0, 0, tiled=True)


def swap_cores(array):
    return lax.ppermute(array, "co", [(0, 1), (1, 0)])


def gather_x(block):
    return jnp.stack([block] + [lax.ppermute(block, "x", [((x + k) % 4, x) for x in range(4)]) for k in (1, 2, 3)])


def flip_pairs():
    pairs = []
    for i in range(16):
        for k in range(8):
            pairs.append((i * 8 + k, (k * 2 + i % 2) * 8 + i // 2))
    return pairs


VMEM = pl.BlockSpec(memory_space=pltpu.VMEM)
SMEM = pl.BlockSpec(memory_space=pltpu.SMEM)


def whole(*shape):
    return pl.BlockSpec(shape, lambda t: (0,) * len(shape))


def fixed(*shape):
    return pl.BlockSpec(shape, lambda t, w: (0,) * len(shape))


def rotate(at, core, first, final, other, vectors, *done):
    mixing = pl.BlockSpec((8, 32, 128), lambda t: (0, 8 + at + t, 0))
    tile = pl.BlockSpec((1024, 256), lambda t: (0, at + t))
    return call(
        rotate_kernel,
        f32(1024, 1024),
        3,
        60,
        grid=(2,),
        in_specs=[SMEM, whole(1024, 768), mixing, mixing, tile] + [pl.BlockSpec(memory_space=pl.ANY)] * len(done),
        out_specs=tile,
        input_output_aliases={5: 0} if done else {},
    )(core, first, final, other, vectors, *done)


def body(matrix, vectors):
    rows_here = matrix.shape[0]
    row_index = lax.axis_index(ROW)
    col_index = lax.axis_index(COL)
    core = lax.axis_index("co").astype(jnp.int32).reshape(1)
    where = jnp.stack([core[0], lax.axis_index("x").astype(jnp.int32), lax.axis_index("zh").astype(jnp.int32)])
    there = flip_pairs()
    back = [(b, a) for a, b in there]

    global_rows = row_index * rows_here + jnp.arange(rows_here, dtype=jnp.int32)
    columns = jnp.where(global_rows[:, None] >= B, matrix[:, :B], F32(0.0))
    parts = {0: columns[:128]}
    for k in ORDER[1:]:
        parts[k] = lax.ppermute(columns[k * 128 : (k + 1) * 128], COL, [(0, k)])
    sent, turned = call(
        choose_kernel, (f32(8, 128, 256), f32(256, 128)), 1, in_specs=[SMEM] + [VMEM] * 8
    )(col_index.astype(jnp.int32).reshape(1), *(parts[k] for k in ORDER))
    turned = lax.ppermute(turned, ALL, there)
    panel_rows = exchange(sent, COL).reshape(1024, B)
    sent = call(gram_kernel, f32(8, 320, 128), 2, 12)(panel_rows, turned)
    panel = exchange(sent, CHIPS)
    half = pl.BlockSpec((8, 384, 128), lambda t, core: (0, 0, 0))
    give, keep = call(
        product_kernel,
        (f32(8, 384, 128), f32(8, 384, 128)),
        12,
        60,
        grid_spec=pltpu.PrefetchScalarGridSpec(
            num_scalar_prefetch=1,
            grid=(4,),
            in_specs=[
                pl.BlockSpec((1024, 256), lambda t, core: (0, 0)),
                pl.BlockSpec((1024, 256), lambda t, core: (0, (1 - core[0]) * 4 + t)),
                pl.BlockSpec((1024, 256), lambda t, core: (0, core[0] * 4 + t)),
                pl.BlockSpec((1024, 256), lambda t, core: (0, t)),
            ],
            out_specs=(half, half),
            scratch_shapes=[pltpu.VMEM((512, 1024), BF16)],
        ),
    )(core, panel_rows, matrix, matrix, vectors)
    give, keep, panel, where = lax.optimization_barrier((give, keep, panel, where))
    got = swap_cores(give)
    gram = jnp.sum(panel[:, 256:], axis=0)
    other_gram = swap_cores(gram)
    other_panel = swap_cores(panel)
    came = exchange(call(join_kernel, f32(8, 448, 128), 1, 12)(keep, got, gram, other_gram), CHIPS)

    product, sent, gram = call(reduce_kernel, (f32(128, 256), f32(8, 384, 128), f32(8, 64, 128)), 2, 12)(came)
    final = exchange(sent, CHIPS)
    near = gather_x(lax.ppermute(product, ALL, back))
    ai, t, schur = call(invert_first, (f32(128, 128),) * 3, 9)(gram)
    inverse = call(invert_second, f32(B, B), 9)(ai, t, schur)
    first, near = call(
        scale_kernel, (jax.ShapeDtypeStruct((1024, 768), BF16), f32(4, 128, 256)), 4, 20
    )(panel_rows, near, inverse)
    final, near, first, inverse = lax.optimization_barrier((final, near, first, inverse))
    other = swap_cores(final)
    far = lax.ppermute(near, "zh", [(0, 1), (1, 0)])
    coupling = call(
        coupling_kernel,
        f32(16, 16, 256),
        2,
        grid=(1,),
        in_specs=[
            pl.BlockSpec((8, 256, 128), lambda t: (0, 0, 0)),
            pl.BlockSpec((8, 256, 128), lambda t: (0, 0, 0)),
        ],
        out_specs=whole(16, 16, 256),
    )(panel, final)
    rotated = rotate(0, core, first, final, other, vectors)
    coupling, rotated = lax.optimization_barrier((exchange(coupling, COUPLED), rotated))
    coupling = exchange(call(sum_kernel, f32(16, 16, 256), 1)(coupling), COUPLED)
    rotated = rotate(2, core, first, final, other, vectors, rotated)
    coupling, rotated = lax.optimization_barrier((coupling, rotated))

    mine = pl.BlockSpec((4, 256, 128), lambda t, w: (jnp.clip(t - 2 * w[0], 0, 1), 0, 0))
    theirs = pl.BlockSpec((4, 256, 128), lambda t, w: (jnp.clip(t - 2 * (1 - w[0]), 0, 1), 0, 0))
    piece = fixed(4, 128, 256)
    updated = call(
        update_kernel,
        f32(1024, 2048),
        12,
        60,
        grid_spec=pltpu.PrefetchScalarGridSpec(
            num_scalar_prefetch=1,
            grid=(4,),
            in_specs=[
                fixed(1024, 768), piece, piece, fixed(256, 256), fixed(16, 16, 256), mine, theirs, mine, theirs,
                pl.BlockSpec((1024, 512), lambda t, w: (0, t)),
            ],
            out_specs=pl.BlockSpec((1024, 512), lambda t, w: (0, t)),
            scratch_shapes=[pltpu.VMEM((1024, 1536), BF16), pltpu.VMEM((1024, 256), F32)],
        ),
    )(where, first, near, far, inverse, coupling, final, other, panel, other_panel, matrix)
    return (updated, rotated)


def solution(mesh):
    fine = Mesh(mesh.devices.reshape(4, 2, 2, 4, 2), ALL)
    placed = (P(ROW, COL), P(ROW, COL))
    return jax.shard_map(body, mesh=fine, in_specs=placed, out_specs=placed, check_vma=False)
```
